512 devices in a mesh: grp: 16 (over x, z_hi), blk: 32 (over y, z_lo, core).
Axes of the slice: x: 4, y: 4, z: 16 (z_hi: 4, z_lo: 4; z = z_hi * 4 + z_lo), core: 2. Of those that a mesh axis runs over, the one named last changes fastest.
Arguments:
- raw_blocks: bfloat16 [64, 96, 64, 256], P('blk', 'grp'), may hold values from -1.5 to 1.5
- metric_factor: bfloat16 [256, 256], replicated, may hold values from -0.375 to 0.375
- sig_list: int32 [64, 96], P('blk', 'grp'), may hold values from 0 to 15, as said below
- live_count: int32 [64, 16], P('blk', 'grp'), may hold values from 1 to 6, as said below
Outputs:
- exchange: float32 [4096, 4096], P('blk', 'grp')
The draws below stay inside these ranges and needn't reach their ends.
Inputs may be any that keep to these rules, and one draw needn't show every extreme that they name: `sig_list`: the 6 slots of one row block in one group name distinct orbital blocks. `live_count`: for every group, each aligned run of 2 row blocks holds a row block with all 6 slots live.
All inputs are finite; a program needn't handle non-finite values.
Results may differ from the reference program's by a relative error of at most 0.0011.
Values may be sent and summed in bfloat16 or wider, within the bound.
No kernel may reach another device: no remote copies, remote signals or barrier semaphores. Data moves between devices by JAX's collectives and lax.ppermute only.
A program may use at most 64 MiB of HBM per device.

```python
import jax
import jax.numpy as jnp
from jax import lax

BS = 64
S = 6
MB = 2
NOB_DEV = 16
AUX = 256
NB = 64
N_GRP = 16


def draw_sig_list(key, part):
    scores = jax.random.randint(key, (NB, N_GRP, NOB_DEV), 0, 1048576)
    scores = scores * NOB_DEV + jnp.arange(NOB_DEV, dtype=jnp.int32)[None, None, :]
    order = jnp.argsort(scores, axis=-1, stable=True).astype(jnp.int32)
    return order[:, :, :S].reshape(NB, N_GRP * S)


def draw_live_count(key, part):
    counts = jax.random.randint(jax.random.fold_in(key, 11), (NB, N_GRP), 1, S + 1)
    picked = jax.random.randint(jax.random.fold_in(key, 12), (NB // MB, N_GRP), 0, MB)
    within = (jnp.arange(NB, dtype=jnp.int32) % MB)[:, None]
    full_row = within == jnp.repeat(picked, MB, axis=0)
    return jnp.where(full_row, S, counts).astype(jnp.int32)


def steps_of(rng, extent, cuts, low, largest):
    def one(axis_at, parts):
        heights = jax.random.uniform(jax.random.fold_in(jax.random.fold_in(rng, 6), axis_at), (parts,), jnp.float32, low / len(cuts), largest / len(cuts))
        return jnp.repeat(jnp.exp(heights), extent[axis_at] // parts).reshape((-1,) + (1,) * (len(extent) - axis_at - 1))

    factor_of = one(*cuts[0])
    for cut in cuts[1:]:
        factor_of = factor_of * one(*cut)
    return factor_of


def bell_draw(key, extent, spread, most, cuts=(), kind=jnp.bfloat16):
    values = spread * jax.random.normal(key, extent, jnp.float32)
    if cuts:
        values = values * steps_of(key, extent, cuts, -0.22, 0.18)
    return jnp.clip(values, -most, most).astype(kind)


def setup_inputs(seed: int = 0) -> dict:
    keys = jax.random.split(jax.random.key(seed), 5)
    raw_blocks = bell_draw(keys[0], (NB, N_GRP * S, BS, AUX), 0.25, 1.5, ((0, 32), (1, 16)))
    metric_factor = bell_draw(keys[1], (AUX, AUX), AUX ** -0.5, 0.375)
    sig_list = draw_sig_list(jax.random.fold_in(keys[4], 71), 0)
    live_count = draw_live_count(jax.random.fold_in(keys[4], 71), 0)
    return dict(raw_blocks=raw_blocks, metric_factor=metric_factor, sig_list=sig_list, live_count=live_count)


def reference(raw_blocks, metric_factor, sig_list, live_count):
    block_count = raw_blocks.shape[0]
    slot_index = jnp.arange(N_GRP * S, dtype=jnp.int32)
    group_of = slot_index // S
    live_mask = (slot_index % S)[None, :] < live_count[:, group_of]
    product = jnp.einsum('mjua,ab->mjub', raw_blocks.astype(jnp.float32), metric_factor.astype(jnp.float32), precision=lax.Precision.HIGHEST)
    contracted = (product * live_mask[:, :, None, None].astype(jnp.float32)).astype(jnp.bfloat16)
    total = jnp.zeros((block_count * BS, block_count * BS), jnp.float32)

    def add_group(total, group_index):
        group_x = lax.dynamic_slice_in_dim(contracted, (group_index * S).astype(jnp.int32), S, 1).astype(jnp.float32)
        group_ids = lax.dynamic_slice_in_dim(sig_list, (group_index * S).astype(jnp.int32), S, 1)
        one_hot = (group_ids[:, :, None] == jnp.arange(NOB_DEV, dtype=jnp.int32)[None, None, :]).astype(jnp.float32)
        dense = jnp.einsum('msn,msua->muna', one_hot, group_x, precision=lax.Precision.HIGHEST)
        flat = dense.reshape(block_count * BS, NOB_DEV * AUX)
        partial_sum = jnp.dot(flat, flat.T, precision=lax.Precision.HIGHEST, preferred_element_type=jnp.float32)
        return total + partial_sum, None

    total, unused = lax.scan(add_group, total, jnp.arange(N_GRP, dtype=jnp.int32))
    return 0.25 * total
```

```python
import jax
import jax.numpy as jnp
from jax import lax
from jax.experimental import pallas as pl
from jax.experimental.pallas import tpu as pltpu
from jax.sharding import Mesh, PartitionSpec as P

AXES = ("x", "zh", "y", "zl", "c")
NOB = 16
SLOTS = 6
BS = 64
AUX = 256
RB = 2
HALF = RB * BS
CHIP = 2 * HALF
BODY = RB * SLOTS * BS
PAY = BODY + 16
TILE = HALF + 16
LEVELS = 32000.0
CROSS = (3, 2, 0, 1)
VMEM = pl.BlockSpec(memory_space=pltpu.VMEM)
SMEM = pl.BlockSpec(memory_space=pltpu.SMEM)


def params(mib):
    return pltpu.CompilerParams(vmem_limit_bytes=mib * 1024 * 1024)


def contract_kernel(raw_ref, metric_ref, sig_ref, live_ref, out_ref):
    for m in range(RB):
        for s in range(SLOTS):
            block = m * SLOTS + s
            product = jnp.dot(
                raw_ref[m, s], metric_ref[...], preferred_element_type=jnp.float32
            )
            live = (s < live_ref[m, 0]).astype(jnp.float32)
            out_ref[block * BS : (block + 1) * BS, :] = (product * live).astype(jnp.bfloat16)
    lane = lax.broadcasted_iota(jnp.int32, (16, AUX), 1)
    ids = jnp.zeros((16, AUX), jnp.int32)
    for m in range(RB):
        for s in range(SLOTS):
            ids = jnp.where(lane == m * SLOTS + s, sig_ref[m, s], ids)
    out_ref[BODY:, :] = ids.astype(jnp.float32).astype(jnp.bfloat16)


def encode(values):
    top = jnp.max(jnp.abs(values), axis=0, keepdims=True)
    exponent = jnp.ceil(jnp.log2(jnp.maximum(top, 1e-30)) + 1e-3)
    coded = jnp.round(values * (LEVELS * jnp.exp2(-exponent)))
    return coded.astype(jnp.int32).astype(jnp.int16), exponent.astype(jnp.int32).astype(jnp.int16)


def decode(ref, index):
    exponent = ref[index + (slice(HALF, TILE), slice(None))].astype(jnp.int32).astype(jnp.float32)
    scale = jnp.exp2(exponent[0:1, :]) * (1.0 / LEVELS)
    return ref[index + (slice(0, HALF), slice(None))].astype(jnp.int32).astype(jnp.float32) * scale


def store_tile(ref, index, values, first, width):
    coded, exponent = encode(values)
    lanes = slice(first, first + width)
    ref[index + (slice(0, HALF), lanes)] = coded
    ref[index + (slice(HALF, TILE), lanes)] = jnp.broadcast_to(exponent, (16, width))


def pairs_kernel(place_ref, ids_ref, *refs):
    mine, other, out_ref, left, column, across = refs[:6], refs[6:11], *refs[11:]
    y, core = place_ref[0], place_ref[1]
    left[...] = jnp.zeros_like(left)
    column[...] = jnp.zeros_like(column)
    across[...] = jnp.zeros_like(across)

    def scatter(src, ids_row, targets):
        for m in range(RB):
            for s in range(SLOTS):
                block = m * SLOTS + s
                orbital = ids_ref[ids_row, block]
                values = src[block * BS : (block + 1) * BS, :]
                lanes = pl.ds(pl.multiple_of(orbital * AUX, AUX), AUX)
                for target, first in targets:
                    rows = pl.ds(pl.multiple_of(first + m * BS, BS), BS)
                    target[rows, lanes] = values

    for d in range(4):
        targets = [(column, core * 4 * HALF + d * HALF)]
        scatter(mine[d], d, targets + ([(left, 0)] if d == 0 else []))
        scatter(other[d], 6 + d, [(column, (1 - core) * 4 * HALF + d * HALF)])
    scatter(mine[4], 4, [(across, core * HALF), (left, HALF)])
    scatter(other[4], 10, [(across, (1 - core) * HALF)])
    scatter(mine[5], 5, [(left, 2 * HALF)])

    nt = (((1,), (1,)), ((), ()))
    for j in range(2):
        part = lax.dot_general(
            left[...], column[j * 4 * HALF : (j + 1) * 4 * HALF, :], nt,
            preferred_element_type=jnp.float32,
        )
        for d in range(4):
            at = lax.rem(y + d, 4)
            for t in range(3):
                tile = 2 if t == 1 else (0 if t == 0 else 1)
                store_tile(
                    out_ref, (at, tile),
                    part[t * HALF : (t + 1) * HALF, d * HALF : (d + 1) * HALF], j * HALF, HALF,
                )
    rows = pl.ds(pl.multiple_of(core * 4 * HALF, 4 * HALF), 4 * HALF)
    part = lax.dot_general(column[rows, :], across[...], nt, preferred_element_type=jnp.float32)
    for d in range(4):
        store_tile(
            out_ref, (lax.rem(y + d, 4), 3), part[d * HALF : (d + 1) * HALF, :], 0, CHIP
        )


def middle_kernel(place_ref, in_ref, *outs):
    for r in range(4):
        m = lax.rem(r + 4 - place_ref[2], 4)
        total = decode(in_ref, (0, m))
        for source in range(1, 4):
            total = total + decode(in_ref, (source, m))
        coded, exponent = encode(total)
        outs[r][:HALF, :] = coded
        outs[r][HALF:, :] = jnp.broadcast_to(exponent, (16, CHIP))


def last_kernel(a, b, c, d, out_ref):
    out_ref[...] = 0.25 * (decode(a, ()) + decode(b, ()) + (decode(c, ()) + decode(d, ())))


def index_of(x, zh, y, zl, c):
    return (((x * 4 + zh) * 4 + y) * 4 + zl) * 2 + c


def final_round(r):
    pairs = []
    for x in range(4):
        for s in range(4):
            for y in range(4):
                for z in range(4):
                    kind = (r - s) % 4
                    dest = (
                        (x, z, y, z), (x, z, y, z ^ 1), (x, z, y, CROSS[z]), (y, CROSS[z], x, z)
                    )[kind]
                    for c in range(2):
                        pairs.append((index_of(x, s, y, z, c), index_of(*dest, c)))
    return pairs


def shards(raw_blocks, metric_factor, sig_list, live_count):
    place = jnp.stack([lax.axis_index("y"), lax.axis_index("c"), lax.axis_index("zh")]).astype(jnp.int32)
    own = pl.pallas_call(
        contract_kernel,
        out_shape=jax.ShapeDtypeStruct((PAY, AUX), jnp.bfloat16),
        in_specs=[VMEM, VMEM, SMEM, SMEM],
        out_specs=VMEM,
        compiler_params=params(16),
        name="contract",
    )(raw_blocks, metric_factor, sig_list, live_count)

    across = lax.ppermute(own, "zl", [(CROSS[z], z) for z in range(4)])
    near = lax.ppermute(own, "zl", [(z ^ 1, z) for z in range(4)])
    column = [own] + [lax.ppermute(own, "y", [((i + d) % 4, i) for i in range(4)]) for d in (1, 2, 3)]
    mine = column + [across, near]
    other = [lax.ppermute(a, "c", [(0, 1), (1, 0)]) for a in column + [across]]
    ids = jnp.stack([a[BODY, : RB * SLOTS] for a in mine + other]).astype(jnp.int32)

    tiles = pl.pallas_call(
        pairs_kernel,
        out_shape=jax.ShapeDtypeStruct((4, 4, TILE, CHIP), jnp.int16),
        in_specs=[SMEM, SMEM] + [VMEM] * 11,
        out_specs=VMEM,
        scratch_shapes=[
            pltpu.VMEM((3 * HALF, NOB * AUX), jnp.bfloat16),
            pltpu.VMEM((8 * HALF, NOB * AUX), jnp.bfloat16),
            pltpu.VMEM((CHIP, NOB * AUX), jnp.bfloat16),
        ],
        compiler_params=params(48),
        name="pairs",
    )(place, ids, *mine, *other)
    arrived = lax.all_to_all(tiles, "x", 0, 0, tiled=True)
    coded = jax.ShapeDtypeStruct((TILE, CHIP), jnp.int16)
    messages = pl.pallas_call(
        middle_kernel,
        out_shape=[coded] * 4,
        in_specs=[SMEM, VMEM],
        out_specs=[VMEM] * 4,
        compiler_params=params(16),
        name="middle",
    )(place, arrived)
    received = [lax.ppermute(a, AXES, final_round(r)) for r, a in enumerate(messages)]
    return pl.pallas_call(
        last_kernel,
        out_shape=jax.ShapeDtypeStruct((HALF, CHIP), jnp.float32),
        in_specs=[VMEM] * 4,
        out_specs=VMEM,
        compiler_params=params(16),
        name="last",
    )(*received)


def solution(mesh):
    fine = Mesh(mesh.devices.reshape(4, 4, 4, 4, 2), AXES)
    blk, grp = ("y", "zl", "c"), ("x", "zh")
    placed = (P(blk, grp, None, None), P(), P(blk, grp), P(blk, grp))
    return jax.shard_map(shards, mesh=fine, in_specs=placed, out_specs=P(blk, grp), check_vma=False)
```

```python
import jax
import jax.numpy as jnp
from jax import lax
from jax.experimental import pallas as pl
from jax.experimental.pallas import tpu as pltpu
from jax.sharding import Mesh, PartitionSpec as P

AXES = ("x", "zh", "y", "zl", "c")
NOB = 16
SLOTS = 6
BS = 64
AUX = 256
RB = 2
HALF = RB * BS
CHIP = 2 * HALF
BODY = RB * SLOTS * BS
PAY = BODY + 16
TILE = HALF + 16
LEVELS = 32000.0
CROSS = (3, 2, 0, 1)
VMEM = pl.BlockSpec(memory_space=pltpu.VMEM)
SMEM = pl.BlockSpec(memory_space=pltpu.SMEM)
ANY = pl.BlockSpec(memory_space=pl.ANY)


def params(mib):
    return pltpu.CompilerParams(vmem_limit_bytes=mib * 1024 * 1024)


def contract_kernel(raw_hbm, metric_hbm, sig_ref, live_ref, out_ref, raw_ref, metric_ref, sems):
    copies = [
        pltpu.make_async_copy(metric_hbm, metric_ref, sems.at[0]),
        pltpu.make_async_copy(raw_hbm, raw_ref, sems.at[1]),
    ]
    for copy in copies:
        copy.start()
    lane = lax.broadcasted_iota(jnp.int32, (16, AUX), 1)
    ids = jnp.zeros((16, AUX), jnp.int32)
    for m in range(RB):
        for s in range(SLOTS):
            ids = jnp.where(lane == m * SLOTS + s, sig_ref[m, s], ids)
    out_ref[BODY:, :] = ids.astype(jnp.float32).astype(jnp.bfloat16)
    for copy in copies:
        copy.wait()
    for m in range(RB):
        for s in range(SLOTS):
            block = m * SLOTS + s
            product = jnp.dot(
                raw_ref[m, s], metric_ref[...], preferred_element_type=jnp.float32
            )
            live = (s < live_ref[m, 0]).astype(jnp.float32)
            out_ref[block * BS : (block + 1) * BS, :] = (product * live).astype(jnp.bfloat16)


def encode(values):
    top = jnp.max(jnp.abs(values), axis=0, keepdims=True)
    exponent = jnp.ceil(jnp.log2(jnp.maximum(top, 1e-30)) + 1e-3)
    coded = jnp.round(values * (LEVELS * jnp.exp2(-exponent)))
    return coded.astype(jnp.int32).astype(jnp.int16), exponent.astype(jnp.int32)


def decode(coded, exponents, row):
    scale = jnp.exp2(exponents[row : row + 1, :].astype(jnp.float32)) * (1.0 / LEVELS)
    return coded.astype(jnp.int32).astype(jnp.float32) * scale


def pick_rows(rows, width):
    at = lax.broadcasted_iota(jnp.int32, (16, width), 0)
    block = jnp.zeros((16, width), jnp.int32)
    for i, row in enumerate(rows):
        block = jnp.where(at == i, jnp.broadcast_to(row, (16, width)), block)
    return block


def load_ids(sources, ids_vmem, ids_smem, sem):
    for i, src in enumerate(sources):
        ids = src[BODY:PAY, 0:128].astype(jnp.float32).astype(jnp.int32)
        ids_vmem[i] = ids[0:8, :]
    return pltpu.make_async_copy(ids_vmem, ids_smem, sem)


def scatter(src, ids, row, target, first):
    for m in range(RB):
        for s in range(SLOTS):
            block = m * SLOTS + s
            orbital = ids[row, 0, block]
            lanes = pl.ds(pl.multiple_of(orbital * AUX, AUX), AUX)
            rows = pl.ds(pl.multiple_of(first + m * BS, BS), BS)
            target[rows, lanes] = src[block * BS : (block + 1) * BS, :]


NT = (((1,), (1,)), ((), ()))


def early_kernel(place_ref, *refs):
    column, mine, other = refs[:4], refs[4:6], refs[6:9]
    out_ref, exp_ref, rows, cols, ids_vmem, ids, sem = refs[9:]
    core = place_ref[1]
    copy = load_ids([*column, *mine, *other], ids_vmem, ids, sem)
    copy.start()
    rows[...] = jnp.zeros_like(rows)
    cols[...] = jnp.zeros_like(cols)
    copy.wait()
    for d in range(4):
        scatter(column[d], ids, d, rows, d * HALF)
    for t in range(3):
        at = t * CHIP
        src, row = (column[0], 0) if t == 0 else (mine[t - 1], 3 + t)
        scatter(src, ids, row, cols, at + core * HALF)
        scatter(other[t], ids, 6 + t, cols, at + (1 - core) * HALF)
    for t in range(3):
        part = lax.dot_general(
            rows[...], cols[t * CHIP : (t + 1) * CHIP, :], NT, preferred_element_type=jnp.float32
        )
        for d in range(4):
            coded, exponent = encode(part[d * HALF : (d + 1) * HALF, :])
            out_ref[d, t * HALF : (t + 1) * HALF, :] = coded
            exp_ref[d, t * 8 : (t + 1) * 8, :] = jnp.broadcast_to(exponent, (8, CHIP))


def late_kernel(place_ref, *refs):
    column, far, far_other, early, early_exp = refs[:4], *refs[4:8]
    outs, (rows, cols, ids_vmem, ids, sem) = refs[8:12], refs[12:]
    y, core, x = place_ref[0], place_ref[1], place_ref[2]
    copy = load_ids([*column, far, far_other], ids_vmem, ids, sem)
    copy.start()
    rows[...] = jnp.zeros_like(rows)
    cols[...] = jnp.zeros_like(cols)
    copy.wait()
    for i in range(4):
        scatter(column[i], ids, i, rows, i * HALF)
    scatter(far, ids, 4, cols, core * HALF)
    scatter(far_other, ids, 5, cols, (1 - core) * HALF)
    for r in range(4):
        d = lax.rem(r + 8 - x - y, 4)
        part = lax.dot_general(
            rows[pl.ds(pl.multiple_of(d * HALF, HALF), HALF), :], cols[...], NT,
            preferred_element_type=jnp.float32,
        )
        coded, exponent = encode(part)
        outs[r][: 3 * HALF, :] = early[d]
        outs[r][3 * HALF : 4 * HALF, :] = coded
        before = early_exp[d]
        block = pick_rows([before[0:1], before[8:9], before[16:17], exponent], CHIP)
        outs[r][4 * HALF :, :] = block.astype(jnp.int16)


def middle_kernel(place_ref, *refs):
    sources, out_ref = refs[:4], refs[4]
    exponents = [src[4 * HALF :, :].astype(jnp.int32) for src in sources]
    for t in range(4):
        total = None
        for src, exps in zip(sources, exponents):
            value = decode(src[t * HALF : (t + 1) * HALF, :], exps, t)
            total = value if total is None else total + value
        coded, exponent = encode(total)
        at = place_ref[3 + t]
        out_ref[at, :HALF, :] = coded
        out_ref[at, HALF:, :] = jnp.broadcast_to(exponent, (16, CHIP)).astype(jnp.int16)


def last_kernel(in_ref, out_ref):
    total = None
    for s in range(4):
        value = decode(in_ref[s, :HALF, :], in_ref[s, HALF:, :].astype(jnp.int32), 0)
        total = value if total is None else total + value
    out_ref[...] = 0.25 * total


def index_of(x, y, c):
    return (x * 4 + y) * 2 + c


def plane_round(r):
    pairs = []
    for x in range(4):
        for y in range(4):
            for c in range(2):
                pairs.append((index_of(x, y, c), index_of(y, (r - x) % 4, c)))
    return pairs


def shards(raw_blocks, metric_factor, sig_list, live_count):
    z = lax.axis_index("zl")
    order = jnp.array([[t, t ^ 1, CROSS[t], CROSS[t ^ 1]] for t in range(4)], jnp.int32)[z]
    first = [lax.axis_index("y"), lax.axis_index("c"), lax.axis_index("x")]
    place = jnp.concatenate([jnp.stack(first).astype(jnp.int32), order])
    own = pl.pallas_call(
        contract_kernel,
        out_shape=jax.ShapeDtypeStruct((PAY, AUX), jnp.bfloat16),
        in_specs=[ANY, ANY, SMEM, SMEM],
        out_specs=VMEM,
        scratch_shapes=[
            pltpu.VMEM(raw_blocks.shape, jnp.bfloat16),
            pltpu.VMEM((AUX, AUX), jnp.bfloat16),
            pltpu.SemaphoreType.DMA((2,)),
        ],
        compiler_params=params(56),
        name="contract",
    )(raw_blocks, metric_factor, sig_list, live_count)

    def swap(a):
        return lax.ppermute(a, "c", [(0, 1), (1, 0)])

    flip = [(i ^ 1, i) for i in range(4)]
    across = lax.ppermute(own, "zl", [(CROSS[i], i) for i in range(4)])
    near = lax.ppermute(own, "zl", flip)
    column = [own] + [lax.ppermute(own, "y", [((i + d) % 4, i) for i in range(4)]) for d in (1, 2, 3)]
    far = lax.ppermute(across, "zl", flip)

    def dense(rows):
        return pltpu.VMEM((rows, NOB * AUX), jnp.bfloat16)

    def ids_scratch(count):
        return [
            pltpu.VMEM((count, 8, 128), jnp.int32),
            pltpu.SMEM((count, 8, 128), jnp.int32),
            pltpu.SemaphoreType.DMA,
        ]

    early = pl.pallas_call(
        early_kernel,
        out_shape=[
            jax.ShapeDtypeStruct((4, 3 * HALF, CHIP), jnp.int16),
            jax.ShapeDtypeStruct((4, 24, CHIP), jnp.int32),
        ],
        in_specs=[SMEM] + [VMEM] * 9,
        out_specs=[VMEM] * 2,
        scratch_shapes=[dense(4 * HALF), dense(3 * CHIP)] + ids_scratch(9),
        compiler_params=params(40),
        cost_estimate=pl.CostEstimate(flops=2 * 512 * 768 * 4096, bytes_accessed=4_000_000, transcendentals=0),
        name="early",
    )(place, *column, near, across, swap(own), swap(near), swap(across))
    message = jax.ShapeDtypeStruct((4 * HALF + 16, CHIP), jnp.int16)
    messages = pl.pallas_call(
        late_kernel,
        out_shape=[message] * 4,
        in_specs=[SMEM] + [VMEM] * 8,
        out_specs=[VMEM] * 4,
        scratch_shapes=[dense(4 * HALF), dense(CHIP)] + ids_scratch(6),
        compiler_params=params(40),
        cost_estimate=pl.CostEstimate(flops=2 * 512 * 256 * 4096, bytes_accessed=4_000_000, transcendentals=0),
        name="late",
    )(place, *column, far, swap(far), *early)
    summed = pl.pallas_call(
        middle_kernel,
        out_shape=jax.ShapeDtypeStruct((4, TILE, CHIP), jnp.int16),
        in_specs=[SMEM] + [VMEM] * 4,
        out_specs=VMEM,
        compiler_params=params(16),
        name="middle",
    )(place, *[lax.ppermute(a, ("x", "y", "c"), plane_round(r)) for r, a in enumerate(messages)])
    arrived = lax.all_to_all(summed, "zh", 0, 0, tiled=True)
    return pl.pallas_call(
        last_kernel,
        out_shape=jax.ShapeDtypeStruct((HALF, CHIP), jnp.float32),
        in_specs=[VMEM],
        out_specs=VMEM,
        compiler_params=params(16),
        name="last",
    )(arrived)


def solution(mesh):
    fine = Mesh(mesh.devices.reshape(4, 4, 4, 4, 2), AXES)
    blk, grp = ("y", "zl", "c"), ("x", "zh")
    placed = (P(blk, grp, None, None), P(), P(blk, grp), P(blk, grp))
    return jax.shard_map(shards, mesh=fine, in_specs=placed, out_specs=P(blk, grp), check_vma=False)
```

```python
import jax
import jax.numpy as jnp
from jax import lax
from jax.experimental import pallas as pl
from jax.experimental.pallas import tpu as pltpu
from jax.sharding import Mesh, PartitionSpec as P

AXES = ("x", "zh", "y", "zl", "c")
NOB = 16
SLOTS = 6
BS = 64
AUX = 256
RB = 2
HALF = RB * BS
CHIP = 2 * HALF
BODY = RB * SLOTS * BS
PAY = BODY + 16
TILE = HALF + 16
LEVELS = 32000.0
CROSS = (3, 2, 0, 1)
VMEM = pl.BlockSpec(memory_space=pltpu.VMEM)
SMEM = pl.BlockSpec(memory_space=pltpu.SMEM)
ANY = pl.BlockSpec(memory_space=pl.ANY)


def params(mib):
    return pltpu.CompilerParams(vmem_limit_bytes=mib * 1024 * 1024)


def contract_kernel(raw_hbm, metric_hbm, sig_ref, live_ref, out_ref, raw_ref, metric_ref, sems):
    copies = [
        pltpu.make_async_copy(metric_hbm, metric_ref, sems.at[0]),
        pltpu.make_async_copy(raw_hbm, raw_ref, sems.at[1]),
    ]
    for copy in copies:
        copy.start()
    lane = lax.broadcasted_iota(jnp.int32, (16, AUX), 1)
    ids = jnp.zeros((16, AUX), jnp.int32)
    for m in range(RB):
        for s in range(SLOTS):
            ids = jnp.where(lane == m * SLOTS + s, sig_ref[m, s], ids)
    out_ref[BODY:, :] = ids.astype(jnp.float32).astype(jnp.bfloat16)
    for copy in copies:
        copy.wait()
    for m in range(RB):
        for s in range(SLOTS):
            block = m * SLOTS + s
            product = jnp.dot(
                raw_ref[m, s], metric_ref[...], preferred_element_type=jnp.float32
            )
            live = (s < live_ref[m]).astype(jnp.float32)
            out_ref[block * BS : (block + 1) * BS, :] = (product * live).astype(jnp.bfloat16)


def encode(values):
    top = jnp.max(jnp.abs(values), axis=0, keepdims=True)
    exponent = jnp.ceil(jnp.log2(jnp.maximum(top, 1e-30)) + 1e-3)
    coded = jnp.round(values * (LEVELS * jnp.exp2(-exponent)))
    return coded.astype(jnp.int32).astype(jnp.int16), exponent.astype(jnp.int32)


def decode(coded, exponents, row):
    scale = jnp.exp2(exponents[row : row + 1, :].astype(jnp.float32)) * (1.0 / LEVELS)
    return coded.astype(jnp.int32).astype(jnp.float32) * scale


def pick_rows(rows, width):
    at = lax.broadcasted_iota(jnp.int32, (16, width), 0)
    block = jnp.zeros((16, width), jnp.int32)
    for i, row in enumerate(rows):
        block = jnp.where(at == i, jnp.broadcast_to(row, (16, width)), block)
    return block


def load_ids(sources, ids_vmem, ids_smem, sem):
    for i, src in enumerate(sources):
        ids = src[BODY:PAY, 0:128].astype(jnp.float32).astype(jnp.int32)
        ids_vmem[i] = ids[0:8, :]
    return pltpu.make_async_copy(ids_vmem, ids_smem, sem)


def scatter(src, ids, row, target, first):
    for m in range(RB):
        for s in range(SLOTS):
            block = m * SLOTS + s
            orbital = ids[row, 0, block]
            lanes = pl.ds(pl.multiple_of(orbital * AUX, AUX), AUX)
            rows = pl.ds(pl.multiple_of(first + m * BS, BS), BS)
            target[rows, lanes] = src[block * BS : (block + 1) * BS, :]


NT = (((1,), (1,)), ((), ()))


TYPES = 3
CHUNK = TYPES * HALF + 16


def pairs_kernel(place_ref, *refs):
    column, mine, other = refs[:4], (refs[0], *refs[4:6]), refs[6:9]
    out_ref, rows, cols, ids_vmem, ids, sem = refs[9:]
    y, core = place_ref[0], place_ref[1]
    copy = load_ids([*column, *mine[1:], *other], ids_vmem, ids, sem)
    copy.start()
    rows[...] = jnp.zeros_like(rows)
    cols[...] = jnp.zeros_like(cols)
    copy.wait()
    for d in range(4):
        scatter(column[d], ids, d, cols, lax.rem(y + d, 4) * HALF)
    for t in range(TYPES):
        scatter(mine[t], ids, 0 if t == 0 else 3 + t, rows, t * CHIP + core * HALF)
        scatter(other[t], ids, 6 + t, rows, t * CHIP + (1 - core) * HALF)
    exponents = {}
    for t in range(TYPES):
        part = lax.dot_general(
            rows[t * CHIP : (t + 1) * CHIP, :], cols[...], NT, preferred_element_type=jnp.float32
        )
        for i in range(4):
            for k in range(2):
                coded, exponent = encode(
                    part[k * HALF : (k + 1) * HALF, i * HALF : (i + 1) * HALF]
                )
                out_ref[i * 2 + k, t * HALF : (t + 1) * HALF, :] = coded
                exponents[i, k, t] = exponent
    for i in range(4):
        for k in range(2):
            block = pick_rows([exponents[i, k, t] for t in range(TYPES)], HALF)
            out_ref[i * 2 + k, TYPES * HALF :, :] = block.astype(jnp.int16)


def put(ref, values):
    coded, exponent = encode(values)
    ref[:HALF, :] = coded
    ref[HALF:, :] = jnp.broadcast_to(exponent, (16, values.shape[1])).astype(jnp.int16)


def middle_kernel(place_ref, in_ref, own_ref, near_ref, across_ref, same_ref, swapped_ref):
    core = place_ref[1]
    for t, ref in enumerate((own_ref, near_ref, across_ref)):
        halves = []
        for k in range(2):
            total = None
            for x in range(4):
                exps = in_ref[x * 2 + k, TYPES * HALF :, :].astype(jnp.int32)
                value = decode(in_ref[x * 2 + k, t * HALF : (t + 1) * HALF, :], exps, t)
                total = value if total is None else total + value
            halves.append(total)
        put(ref, jnp.concatenate(halves, axis=1))
        if t == 2:
            first = core == 0
            put(same_ref, jnp.where(first, halves[0], halves[1]).T)
            put(swapped_ref, jnp.where(first, halves[1], halves[0]).T)


def cross(z):
    return jnp.where(z < 2, 3 - z, z - 2)


def assemble_kernel(place_ref, own_ref, near_ref, across_ref, same_ref, swapped_ref, out_ref):
    core, z = place_ref[1], place_ref[2]
    flipped = z + 1 - 2 * lax.rem(z, 2)
    out_ref[z] = own_ref[...]
    out_ref[flipped] = near_ref[...]
    out_ref[cross(flipped)] = across_ref[...]
    here = pl.ds(pl.multiple_of(core * HALF, HALF), HALF)
    there = pl.ds(pl.multiple_of((1 - core) * HALF, HALF), HALF)
    out_ref[cross(z), :, here] = same_ref[...]
    out_ref[cross(z), :, there] = swapped_ref[...]


def last_kernel(in_ref, out_ref):
    total = None
    for s in range(4):
        value = decode(in_ref[s, :HALF, :], in_ref[s, HALF:, :].astype(jnp.int32), 0)
        total = value if total is None else total + value
    out_ref[...] = 0.25 * total


def mirror(swap_cores):
    return [
        ((x * 4 + y) * 2 + c, (y * 4 + x) * 2 + (c ^ swap_cores))
        for x in range(4) for y in range(4) for c in range(2)
    ]


def shards(raw_blocks, metric_factor, sig_list, live_count):
    place = jnp.stack([lax.axis_index("y"), lax.axis_index("c"), lax.axis_index("zl")]).astype(jnp.int32)
    own = pl.pallas_call(
        contract_kernel,
        out_shape=jax.ShapeDtypeStruct((PAY, AUX), jnp.bfloat16),
        in_specs=[ANY, ANY, SMEM, SMEM],
        out_specs=VMEM,
        scratch_shapes=[
            pltpu.VMEM(raw_blocks.shape, jnp.bfloat16),
            pltpu.VMEM((AUX, AUX), jnp.bfloat16),
            pltpu.SemaphoreType.DMA((2,)),
        ],
        compiler_params=params(24),
        name="contract",
    )(raw_blocks, metric_factor, sig_list, live_count.reshape(RB))

    def swap(a):
        return lax.ppermute(a, "c", [(0, 1), (1, 0)])

    flip = [(i ^ 1, i) for i in range(4)]
    across = lax.ppermute(own, "zl", [(CROSS[i], i) for i in range(4)])
    near = lax.ppermute(own, "zl", flip)
    column = [own] + [lax.ppermute(own, "y", [((i + d) % 4, i) for i in range(4)]) for d in (1, 2, 3)]
    tiles = pl.pallas_call(
        pairs_kernel,
        out_shape=jax.ShapeDtypeStruct((8, CHUNK, HALF), jnp.int16),
        in_specs=[SMEM] + [VMEM] * 9,
        out_specs=VMEM,
        scratch_shapes=[
            pltpu.VMEM((TYPES * CHIP, NOB * AUX), jnp.bfloat16),
            pltpu.VMEM((4 * HALF, NOB * AUX), jnp.bfloat16),
            pltpu.VMEM((9, 8, 128), jnp.int32),
            pltpu.SMEM((9, 8, 128), jnp.int32),
            pltpu.SemaphoreType.DMA,
        ],
        compiler_params=params(40),
        name="pairs",
    )(place, *column, near, across, swap(own), swap(near), swap(across))
    arrived = lax.all_to_all(tiles, ("x", "c"), 0, 0, tiled=True)
    wide = jax.ShapeDtypeStruct((TILE, CHIP), jnp.int16)
    narrow = jax.ShapeDtypeStruct((TILE, HALF), jnp.int16)
    own_tile, near_tile, across_tile, same, swapped = pl.pallas_call(
        middle_kernel,
        out_shape=[wide] * 3 + [narrow] * 2,
        in_specs=[SMEM, VMEM],
        out_specs=[VMEM] * 5,
        compiler_params=params(16),
        name="middle",
    )(place, arrived)
    ordered = pl.pallas_call(
        assemble_kernel,
        out_shape=jax.ShapeDtypeStruct((4, TILE, CHIP), jnp.int16),
        in_specs=[SMEM] + [VMEM] * 5,
        out_specs=VMEM,
        compiler_params=params(16),
        name="assemble",
    )(
        place,
        own_tile,
        lax.ppermute(near_tile, "zl", flip),
        lax.ppermute(across_tile, "zl", [(i, CROSS[i]) for i in range(4)]),
        lax.ppermute(same, ("x", "y", "c"), mirror(0)),
        lax.ppermute(swapped, ("x", "y", "c"), mirror(1)),
    )
    arrived = lax.all_to_all(ordered, "zh", 0, 0, tiled=True)
    return pl.pallas_call(
        last_kernel,
        out_shape=jax.ShapeDtypeStruct((HALF, CHIP), jnp.float32),
        in_specs=[VMEM],
        out_specs=VMEM,
        compiler_params=params(16),
        name="last",
    )(arrived)


def solution(mesh):
    fine = Mesh(mesh.devices.reshape(4, 4, 4, 4, 2), AXES)
    blk, grp = ("y", "zl", "c"), ("x", "zh")
    placed = (P(blk, grp, None, None), P(), P(blk, grp), P(blk, grp))
    return jax.shard_map(shards, mesh=fine, in_specs=placed, out_specs=P(blk, grp), check_vma=False)
```

```python
import jax
import jax.numpy as jnp
from jax import lax
from jax.experimental import pallas as pl
from jax.experimental.pallas import tpu as pltpu
from jax.sharding import Mesh, PartitionSpec as P

AXES = ("x", "zh", "y", "zl", "c")
NOB = 16
SLOTS = 6
BS = 64
AUX = 256
RB = 2
HALF = RB * BS
CHIP = 2 * HALF
BODY = RB * SLOTS * BS
PAY = BODY + 16
TILE = HALF + 16
LEVELS = 32000.0
CROSS = (3, 2, 0, 1)
VMEM = pl.BlockSpec(memory_space=pltpu.VMEM)
SMEM = pl.BlockSpec(memory_space=pltpu.SMEM)
ANY = pl.BlockSpec(memory_space=pl.ANY)


def params(mib):
    return pltpu.CompilerParams(vmem_limit_bytes=mib * 1024 * 1024)


def contract_kernel(raw_hbm, metric_hbm, sig_ref, live_ref, out_ref, raw_ref, metric_ref, sems):
    copies = [
        pltpu.make_async_copy(metric_hbm, metric_ref, sems.at[0]),
        pltpu.make_async_copy(raw_hbm, raw_ref, sems.at[1]),
    ]
    for copy in copies:
        copy.start()
    lane = lax.broadcasted_iota(jnp.int32, (16, AUX), 1)
    ids = jnp.zeros((16, AUX), jnp.int32)
    for m in range(RB):
        for s in range(SLOTS):
            ids = jnp.where(lane == m * SLOTS + s, sig_ref[m, s], ids)
    out_ref[BODY:, :] = ids.astype(jnp.float32).astype(jnp.bfloat16)
    for copy in copies:
        copy.wait()
    for m in range(RB):
        for s in range(SLOTS):
            block = m * SLOTS + s
            product = jnp.dot(
                raw_ref[m, s], metric_ref[...], preferred_element_type=jnp.float32
            )
            live = (s < live_ref[m]).astype(jnp.float32)
            out_ref[block * BS : (block + 1) * BS, :] = (product * live).astype(jnp.bfloat16)


def encode(values):
    top = jnp.max(jnp.abs(values), axis=0, keepdims=True)
    exponent = jnp.ceil(jnp.log2(jnp.maximum(top, 1e-30)) + 1e-3)
    coded = jnp.round(values * (LEVELS * jnp.exp2(-exponent)))
    return coded.astype(jnp.int32).astype(jnp.int16), exponent.astype(jnp.int32)


def decode(coded, exponents, row):
    scale = jnp.exp2(exponents[row : row + 1, :].astype(jnp.float32)) * (1.0 / LEVELS)
    return coded.astype(jnp.int32).astype(jnp.float32) * scale


def pick_rows(rows, width):
    at = lax.broadcasted_iota(jnp.int32, (16, width), 0)
    block = jnp.zeros((16, width), jnp.int32)
    for i, row in enumerate(rows):
        block = jnp.where(at == i, jnp.broadcast_to(row, (16, width)), block)
    return block


def load_ids(sources, ids_vmem, ids_smem, sem):
    for i, src in enumerate(sources):
        ids = src[BODY:PAY, 0:128].astype(jnp.float32).astype(jnp.int32)
        ids_vmem[i] = ids[0:8, :]
    return pltpu.make_async_copy(ids_vmem, ids_smem, sem)


def scatter(src, ids, row, target, first):
    for m in range(RB):
        for s in range(SLOTS):
            block = m * SLOTS + s
            orbital = ids[row, 0, block]
            lanes = pl.ds(pl.multiple_of(orbital * AUX, AUX), AUX)
            rows = pl.ds(pl.multiple_of(first + m * BS, BS), BS)
            target[rows, lanes] = src[block * BS : (block + 1) * BS, :]


NT = (((1,), (1,)), ((), ()))


TYPES = 3
CHUNK = 2 * CHIP + 16
WIDE = CHIP + 16


def column_kernel(place_ref, *refs):
    column, (out_ref, ids_vmem, ids, sem) = refs[:4], refs[4:]
    copy = load_ids(column, ids_vmem, ids, sem)
    copy.start()
    out_ref[...] = jnp.zeros_like(out_ref)
    copy.wait()
    for i, d in enumerate((0, 2, 1, 3)):
        scatter(column[i], ids, i, out_ref, lax.rem(place_ref[0] + d, 4) * HALF)


def pairs_kernel(place_ref, *refs):
    cols, *wide = refs[:4]
    out_ref, rows, ids_vmem, ids, sem = refs[4:]
    core = place_ref[1]
    halves = [src.at[k] for src in wide for k in range(2)]
    copy = load_ids(halves, ids_vmem, ids, sem)
    copy.start()
    rows[...] = jnp.zeros_like(rows)
    copy.wait()
    for i, t in enumerate((0, 2 - core, 1 + core)):
        for k in range(2):
            scatter(halves[i * 2 + k], ids, i * 2 + k, rows, t * CHIP + k * HALF)
    exponents = {}
    for t in range(TYPES):
        part = lax.dot_general(
            rows[t * CHIP : (t + 1) * CHIP, :], cols[...], NT, preferred_element_type=jnp.float32
        )
        for i in range(4):
            coded, exponents[t, i] = encode(part[:, i * HALF : (i + 1) * HALF])
            chunk, first = i * 2 + t // 2, (t % 2) * CHIP
            out_ref[chunk, first : first + CHIP, :] = coded
    for i in range(4):
        out_ref[i * 2 + 1, CHIP : 2 * CHIP, :] = jnp.zeros((CHIP, HALF), jnp.int16)
        for k in range(2):
            block = pick_rows([exponents[k * 2, i], exponents[1, i]], HALF)
            out_ref[i * 2 + k, 2 * CHIP :, :] = block.astype(jnp.int16)


def middle_kernel(place_ref, in_ref, even_ref, odd_ref):
    tiles = []
    for u in range(2):
        halves = []
        for k in range(2):
            total = None
            for x in range(4):
                exps = in_ref[x * 2 + k, 2 * CHIP :, :].astype(jnp.int32)
                value = decode(in_ref[x * 2 + k, u * CHIP : (u + 1) * CHIP, :], exps, u)
                total = value if total is None else total + value
            halves.append(total)
        tiles.append(jnp.concatenate(halves, axis=1))
    first = encode(tiles[0])
    second = encode(jnp.where(place_ref[1] == 0, tiles[1], tiles[0].T))

    def write(ref, pair):
        ref[:CHIP, :] = pair[0]
        ref[CHIP:, :] = jnp.broadcast_to(pair[1], (16, CHIP)).astype(jnp.int16)

    even = lax.rem(place_ref[2], 2) == 0

    @pl.when(even)
    def _():
        write(even_ref, first)
        write(odd_ref, second)

    @pl.when(jnp.logical_not(even))
    def _():
        write(even_ref, second)
        write(odd_ref, first)


def join_kernel(place_ref, a_ref, b_ref, keep_ref, send_ref):
    core = place_ref[1]
    for ref, half in ((keep_ref, core), (send_ref, 1 - core)):
        rows = pl.ds(pl.multiple_of(half * HALF, HALF), HALF)
        ref[...] = sum(
            decode(src[rows, :], src[CHIP:, :].astype(jnp.int32), 0) for src in (a_ref, b_ref)
        )


def last_kernel(keep_ref, come_ref, out_ref):
    out_ref[...] = 0.25 * (keep_ref[...] + come_ref[...])


def index_of(x, zh, y, zl, c):
    return (((x * 4 + zh) * 4 + y) * 4 + zl) * 2 + c


def far_round(r):
    pairs = []
    for x in range(4):
        for s in range(4):
            for y in range(4):
                for z in range(4):
                    kinds = (
                        ((x, z, y, z), (x, z, y, z ^ 1)),
                        ((x, z, y, CROSS[z]), (y, CROSS[z], x, z)),
                    )
                    for c in range(2):
                        dest = kinds[c][(s + r) % 2]
                        pairs.append((index_of(x, s, y, z, c), index_of(*dest, s // 2)))
    return pairs


def shards(raw_blocks, metric_factor, sig_list, live_count):
    place = jnp.stack([lax.axis_index("y"), lax.axis_index("c"), lax.axis_index("zh")]).astype(jnp.int32)
    own = pl.pallas_call(
        contract_kernel,
        out_shape=jax.ShapeDtypeStruct((PAY, AUX), jnp.bfloat16),
        in_specs=[ANY, ANY, SMEM, SMEM],
        out_specs=VMEM,
        scratch_shapes=[
            pltpu.VMEM(raw_blocks.shape, jnp.bfloat16),
            pltpu.VMEM((AUX, AUX), jnp.bfloat16),
            pltpu.SemaphoreType.DMA((2,)),
        ],
        compiler_params=params(24),
        name="contract",
    )(raw_blocks, metric_factor, sig_list, live_count.reshape(RB))

    def swap(a):
        return lax.ppermute(a, "c", [(0, 1), (1, 0)])

    both = lax.all_gather(own, "c")
    along = lax.ppermute(
        both,
        ("zl", "c"),
        [(CROSS[i] * 2, i * 2) for i in range(4)] + [((i ^ 1) * 2 + 1, i * 2 + 1) for i in range(4)],
    )
    column = [own] + [lax.ppermute(own, "y", [((i + d) % 4, i) for i in range(4)]) for d in (2, 1, 3)]
    dense = pl.pallas_call(
        column_kernel,
        out_shape=jax.ShapeDtypeStruct((4 * HALF, NOB * AUX), jnp.bfloat16),
        in_specs=[SMEM] + [VMEM] * 4,
        out_specs=VMEM,
        scratch_shapes=[
            pltpu.VMEM((4, 8, 128), jnp.int32),
            pltpu.SMEM((4, 8, 128), jnp.int32),
            pltpu.SemaphoreType.DMA,
        ],
        compiler_params=params(16),
        cost_estimate=pl.CostEstimate(flops=20_000_000_000, bytes_accessed=6_000_000, transcendentals=0),
        name="column",
    )(place, *column)
    tiles = pl.pallas_call(
        pairs_kernel,
        out_shape=jax.ShapeDtypeStruct((8, CHUNK, HALF), jnp.int16),
        in_specs=[SMEM] + [VMEM] * 4,
        out_specs=VMEM,
        scratch_shapes=[
            pltpu.VMEM((TYPES * CHIP, NOB * AUX), jnp.bfloat16),
            pltpu.VMEM((6, 8, 128), jnp.int32),
            pltpu.SMEM((6, 8, 128), jnp.int32),
            pltpu.SemaphoreType.DMA,
        ],
        compiler_params=params(24),
        name="pairs",
    )(place, dense, both, along, swap(along))
    arrived = lax.all_to_all(tiles, ("x", "c"), 0, 0, tiled=True)
    wide = jax.ShapeDtypeStruct((WIDE, CHIP), jnp.int16)
    messages = pl.pallas_call(
        middle_kernel,
        out_shape=[wide] * 2,
        in_specs=[SMEM, VMEM],
        out_specs=[VMEM] * 2,
        compiler_params=params(24),
        name="middle",
    )(place, arrived)
    half = jax.ShapeDtypeStruct((HALF, CHIP), jnp.float32)
    keep, send = pl.pallas_call(
        join_kernel,
        out_shape=[half] * 2,
        in_specs=[SMEM, VMEM, VMEM],
        out_specs=[VMEM] * 2,
        compiler_params=params(16),
        name="join",
    )(place, *[lax.ppermute(a, AXES, far_round(r)) for r, a in enumerate(messages)])
    return pl.pallas_call(
        last_kernel,
        out_shape=half,
        in_specs=[VMEM] * 2,
        out_specs=VMEM,
        compiler_params=params(16),
        name="last",
    )(keep, swap(send))


def solution(mesh):
    fine = Mesh(mesh.devices.reshape(4, 4, 4, 4, 2), AXES)
    blk, grp = ("y", "zl", "c"), ("x", "zh")
    placed = (P(blk, grp, None, None), P(), P(blk, grp), P(blk, grp))
    return jax.shard_map(shards, mesh=fine, in_specs=placed, out_specs=P(blk, grp), check_vma=False)
```

```python
import jax
import jax.numpy as jnp
from jax import lax
from jax.experimental import pallas as pl
from jax.experimental.pallas import tpu as pltpu
from jax.sharding import Mesh, PartitionSpec as P

AXES = ("x", "zh", "y", "zl", "c")
NOB = 16
SLOTS = 6
BS = 64
AUX = 256
RB = 2
HALF = RB * BS
CHIP = 2 * HALF
BODY = RB * SLOTS * BS
PAY = BODY + 16
TILE = HALF + 16
LEVELS = 32000.0
CROSS = (3, 2, 0, 1)
VMEM = pl.BlockSpec(memory_space=pltpu.VMEM)
SMEM = pl.BlockSpec(memory_space=pltpu.SMEM)
ANY = pl.BlockSpec(memory_space=pl.ANY)


def params(mib):
    return pltpu.CompilerParams(vmem_limit_bytes=mib * 1024 * 1024)


def contract_kernel(raw_hbm, metric_hbm, sig_ref, live_ref, out_ref, raw_ref, metric_ref, sems):
    copies = [
        pltpu.make_async_copy(metric_hbm, metric_ref, sems.at[0]),
        pltpu.make_async_copy(raw_hbm, raw_ref, sems.at[1]),
    ]
    for copy in copies:
        copy.start()
    lane = lax.broadcasted_iota(jnp.int32, (16, AUX), 1)
    ids = jnp.zeros((16, AUX), jnp.int32)
    for m in range(RB):
        for s in range(SLOTS):
            ids = jnp.where(lane == m * SLOTS + s, sig_ref[m, s], ids)
    out_ref[BODY:, :] = ids.astype(jnp.float32).astype(jnp.bfloat16)
    for copy in copies:
        copy.wait()
    for m in range(RB):
        for s in range(SLOTS):
            block = m * SLOTS + s
            product = jnp.dot(
                raw_ref[m, s], metric_ref[...], preferred_element_type=jnp.float32
            )
            live = (s < live_ref[m]).astype(jnp.float32)
            out_ref[block * BS : (block + 1) * BS, :] = (product * live).astype(jnp.bfloat16)


def encode(values):
    top = jnp.max(jnp.abs(values), axis=0, keepdims=True)
    exponent = jnp.ceil(jnp.log2(jnp.maximum(top, 1e-30)) + 1e-3)
    coded = jnp.round(values * (LEVELS * jnp.exp2(-exponent)))
    return coded.astype(jnp.int32).astype(jnp.int16), exponent.astype(jnp.int32)


def decode(coded, exponents, row):
    scale = jnp.exp2(exponents[row : row + 1, :].astype(jnp.float32)) * (1.0 / LEVELS)
    return coded.astype(jnp.int32).astype(jnp.float32) * scale


def pick_rows(rows, width):
    at = lax.broadcasted_iota(jnp.int32, (16, width), 0)
    block = jnp.zeros((16, width), jnp.int32)
    for i, row in enumerate(rows):
        block = jnp.where(at == i, jnp.broadcast_to(row, (16, width)), block)
    return block


def load_ids(sources, ids_vmem, ids_smem, sem):
    for i, src in enumerate(sources):
        ids = src[BODY:PAY, 0:128].astype(jnp.float32).astype(jnp.int32)
        ids_vmem[i] = ids[0:8, :]
    return pltpu.make_async_copy(ids_vmem, ids_smem, sem)


def scatter(src, ids, row, target, first):
    for m in range(RB):
        for s in range(SLOTS):
            block = m * SLOTS + s
            orbital = ids[row, 0, block]
            lanes = pl.ds(pl.multiple_of(orbital * AUX, AUX), AUX)
            rows = pl.ds(pl.multiple_of(first + m * BS, BS), BS)
            target[rows, lanes] = src[block * BS : (block + 1) * BS, :]


NT = (((1,), (1,)), ((), ()))


TYPES = 3
CHUNK = 2 * CHIP + 16
WIDE = CHIP + 16


def column_kernel(place_ref, *refs):
    column, (out_ref, ids_vmem, ids, sem) = refs[:4], refs[4:]
    copy = load_ids(column, ids_vmem, ids, sem)
    copy.start()
    out_ref[...] = jnp.zeros_like(out_ref)
    copy.wait()
    for i, d in enumerate((0, 2, 1, 3)):
        scatter(column[i], ids, i, out_ref, lax.rem(place_ref[0] + d, 4) * HALF)


def rows_kernel(src, out_ref, ids_vmem, ids, sem):
    halves = [src.at[k] for k in range(2)]
    copy = load_ids(halves, ids_vmem, ids, sem)
    copy.start()
    out_ref[...] = jnp.zeros_like(out_ref)
    copy.wait()
    for k in range(2):
        scatter(halves[k], ids, k, out_ref, k * HALF)


def pairs_kernel(place_ref, cols, own_rows, first_rows, src, out_ref, rows, ids_vmem, ids, sem):
    core = place_ref[1]
    rows_kernel(src, rows, ids_vmem, ids, sem)
    exponents = {}
    places = ((0, 0), (1 - core, core * CHIP), (core, (1 - core) * CHIP))
    for t, block in enumerate((own_rows, first_rows, rows)):
        part = lax.dot_general(block[...], cols[...], NT, preferred_element_type=jnp.float32)
        chunk, first = places[t]
        for i in range(4):
            coded, exponents[t, i] = encode(part[:, i * HALF : (i + 1) * HALF])
            at = pl.ds(first if t == 0 else pl.multiple_of(first, CHIP), CHIP)
            out_ref[i * 2 + chunk, at, :] = coded
    zero = core == 0
    for i in range(4):
        out_ref[i * 2 + 1, CHIP : 2 * CHIP, :] = jnp.zeros((CHIP, HALF), jnp.int16)
        near = jnp.where(zero, exponents[2, i], exponents[1, i])
        across = jnp.where(zero, exponents[1, i], exponents[2, i])
        out_ref[i * 2, 2 * CHIP :, :] = pick_rows([exponents[0, i], near], HALF).astype(jnp.int16)
        out_ref[i * 2 + 1, 2 * CHIP :, :] = pick_rows([across], HALF).astype(jnp.int16)


def middle_kernel(place_ref, in_ref, even_ref, odd_ref):
    tiles = []
    for u in range(2):
        halves = []
        for k in range(2):
            total = None
            for x in range(4):
                exps = in_ref[x * 2 + k, 2 * CHIP :, :].astype(jnp.int32)
                value = decode(in_ref[x * 2 + k, u * CHIP : (u + 1) * CHIP, :], exps, u)
                total = value if total is None else total + value
            halves.append(total)
        tiles.append(jnp.concatenate(halves, axis=1))
    first = encode(tiles[0])
    second = encode(jnp.where(place_ref[1] == 0, tiles[1], tiles[0].T))

    def write(ref, pair):
        ref[:CHIP, :] = pair[0]
        ref[CHIP:, :] = jnp.broadcast_to(pair[1], (16, CHIP)).astype(jnp.int16)

    even = lax.rem(place_ref[2], 2) == 0

    @pl.when(even)
    def _():
        write(even_ref, first)
        write(odd_ref, second)

    @pl.when(jnp.logical_not(even))
    def _():
        write(even_ref, second)
        write(odd_ref, first)


def join_kernel(place_ref, a_ref, b_ref, keep_ref, send_ref):
    core = place_ref[1]
    for ref, half in ((keep_ref, core), (send_ref, 1 - core)):
        rows = pl.ds(pl.multiple_of(half * HALF, HALF), HALF)
        ref[...] = sum(
            decode(src[rows, :], src[CHIP:, :].astype(jnp.int32), 0) for src in (a_ref, b_ref)
        )


def last_kernel(keep_ref, come_ref, out_ref):
    out_ref[...] = 0.25 * (keep_ref[...] + come_ref[...])


def index_of(x, zh, y, zl, c):
    return (((x * 4 + zh) * 4 + y) * 4 + zl) * 2 + c


def far_round(r):
    pairs = []
    for x in range(4):
        for s in range(4):
            for y in range(4):
                for z in range(4):
                    kinds = (
                        ((x, z, y, z), (x, z, y, z ^ 1)),
                        ((x, z, y, CROSS[z]), (y, CROSS[z], x, z)),
                    )
                    for c in range(2):
                        dest = kinds[c][(s + r) % 2]
                        pairs.append((index_of(x, s, y, z, c), index_of(*dest, s // 2)))
    return pairs


def shards(raw_blocks, metric_factor, sig_list, live_count):
    place = jnp.stack([lax.axis_index("y"), lax.axis_index("c"), lax.axis_index("zh")]).astype(jnp.int32)
    own = pl.pallas_call(
        contract_kernel,
        out_shape=jax.ShapeDtypeStruct((PAY, AUX), jnp.bfloat16),
        in_specs=[ANY, ANY, SMEM, SMEM],
        out_specs=VMEM,
        scratch_shapes=[
            pltpu.VMEM(raw_blocks.shape, jnp.bfloat16),
            pltpu.VMEM((AUX, AUX), jnp.bfloat16),
            pltpu.SemaphoreType.DMA((2,)),
        ],
        compiler_params=params(56),
        name="contract",
    )(raw_blocks, metric_factor, sig_list, live_count.reshape(RB))

    def swap(a):
        return lax.ppermute(a, "c", [(0, 1), (1, 0)])

    both = lax.all_gather(own, "c")
    along = lax.ppermute(
        both,
        ("zl", "c"),
        [(CROSS[i] * 2, i * 2) for i in range(4)] + [((i ^ 1) * 2 + 1, i * 2 + 1) for i in range(4)],
    )
    column = [own] + [lax.ppermute(own, "y", [((i + d) % 4, i) for i in range(4)]) for d in (2, 1, 3)]
    def ids_scratch(count):
        return [
            pltpu.VMEM((count, 8, 128), jnp.int32),
            pltpu.SMEM((count, 8, 128), jnp.int32),
            pltpu.SemaphoreType.DMA,
        ]

    def dense_rows(block):
        return pl.pallas_call(
            rows_kernel,
            out_shape=jax.ShapeDtypeStruct((CHIP, NOB * AUX), jnp.bfloat16),
            in_specs=[VMEM],
            out_specs=VMEM,
            scratch_shapes=ids_scratch(2),
            compiler_params=params(16),
            cost_estimate=pl.CostEstimate(flops=1_000_000_000, bytes_accessed=3_000_000, transcendentals=0),
            name="rows",
        )(block)

    dense = pl.pallas_call(
        column_kernel,
        out_shape=jax.ShapeDtypeStruct((4 * HALF, NOB * AUX), jnp.bfloat16),
        in_specs=[SMEM] + [VMEM] * 4,
        out_specs=VMEM,
        scratch_shapes=ids_scratch(4),
        compiler_params=params(16),
        cost_estimate=pl.CostEstimate(flops=20_000_000_000, bytes_accessed=6_000_000, transcendentals=0),
        name="column",
    )(place, *column)
    tiles = pl.pallas_call(
        pairs_kernel,
        out_shape=jax.ShapeDtypeStruct((8, CHUNK, HALF), jnp.int16),
        in_specs=[SMEM] + [VMEM] * 4,
        out_specs=VMEM,
        scratch_shapes=[pltpu.VMEM((CHIP, NOB * AUX), jnp.bfloat16)] + ids_scratch(2),
        compiler_params=params(16),
        name="pairs",
    )(place, dense, dense_rows(both), dense_rows(along), swap(along))
    arrived = lax.all_to_all(tiles, ("x", "c"), 0, 0, tiled=True)
    wide = jax.ShapeDtypeStruct((WIDE, CHIP), jnp.int16)
    messages = pl.pallas_call(
        middle_kernel,
        out_shape=[wide] * 2,
        in_specs=[SMEM, VMEM],
        out_specs=[VMEM] * 2,
        compiler_params=params(24),
        name="middle",
    )(place, arrived)
    half = jax.ShapeDtypeStruct((HALF, CHIP), jnp.float32)
    keep, send = pl.pallas_call(
        join_kernel,
        out_shape=[half] * 2,
        in_specs=[SMEM, VMEM, VMEM],
        out_specs=[VMEM] * 2,
        compiler_params=params(16),
        name="join",
    )(place, *[lax.ppermute(a, AXES, far_round(r)) for r, a in enumerate(messages)])
    return pl.pallas_call(
        last_kernel,
        out_shape=half,
        in_specs=[VMEM] * 2,
        out_specs=VMEM,
        compiler_params=params(16),
        name="last",
    )(keep, swap(send))


def solution(mesh):
    fine = Mesh(mesh.devices.reshape(4, 4, 4, 4, 2), AXES)
    blk, grp = ("y", "zl", "c"), ("x", "zh")
    placed = (P(blk, grp, None, None), P(), P(blk, grp), P(blk, grp))
    return jax.shard_map(shards, mesh=fine, in_specs=placed, out_specs=P(blk, grp), check_vma=False)
```

```python
import jax
import jax.numpy as jnp
from jax import lax
from jax.experimental import pallas as pl
from jax.experimental.pallas import tpu as pltpu
from jax.sharding import Mesh, PartitionSpec as P

AXES = ("x", "zh", "y", "zl", "c")
NOB = 16
SLOTS = 6
BS = 64
AUX = 256
RB = 2
HALF = RB * BS
CHIP = 2 * HALF
BODY = RB * SLOTS * BS
PAY = BODY + 16
TILE = HALF + 16
LEVELS = 32000.0
CROSS = (3, 2, 0, 1)
VMEM = pl.BlockSpec(memory_space=pltpu.VMEM)
SMEM = pl.BlockSpec(memory_space=pltpu.SMEM)
ANY = pl.BlockSpec(memory_space=pl.ANY)


def params(mib):
    return pltpu.CompilerParams(vmem_limit_bytes=mib * 1024 * 1024)


def contract_kernel(raw_hbm, metric_hbm, sig_ref, live_ref, out_ref, raw_ref, metric_ref, sems):
    copies = [
        pltpu.make_async_copy(metric_hbm, metric_ref, sems.at[0]),
        pltpu.make_async_copy(raw_hbm, raw_ref, sems.at[1]),
    ]
    for copy in copies:
        copy.start()
    lane = lax.broadcasted_iota(jnp.int32, (16, AUX), 1)
    ids = jnp.zeros((16, AUX), jnp.int32)
    for m in range(RB):
        for s in range(SLOTS):
            ids = jnp.where(lane == m * SLOTS + s, sig_ref[m, s], ids)
    out_ref[BODY:, :] = ids.astype(jnp.float32).astype(jnp.bfloat16)
    for copy in copies:
        copy.wait()
    for m in range(RB):
        for s in range(SLOTS):
            block = m * SLOTS + s
            product = jnp.dot(
                raw_ref[m, s], metric_ref[...], preferred_element_type=jnp.float32
            )
            live = (s < live_ref[m]).astype(jnp.float32)
            out_ref[block * BS : (block + 1) * BS, :] = (product * live).astype(jnp.bfloat16)


def encode(values):
    top = jnp.max(jnp.abs(values), axis=0, keepdims=True)
    exponent = jnp.ceil(jnp.log2(jnp.maximum(top, 1e-30)) + 1e-3)
    coded = jnp.round(values * (LEVELS * jnp.exp2(-exponent)))
    return coded.astype(jnp.int32).astype(jnp.int16), exponent.astype(jnp.int32)


def decode(coded, exponents, row):
    scale = jnp.exp2(exponents[row : row + 1, :].astype(jnp.float32)) * (1.0 / LEVELS)
    return coded.astype(jnp.int32).astype(jnp.float32) * scale


def pick_rows(rows, width):
    at = lax.broadcasted_iota(jnp.int32, (16, width), 0)
    block = jnp.zeros((16, width), jnp.int32)
    for i, row in enumerate(rows):
        block = jnp.where(at == i, jnp.broadcast_to(row, (16, width)), block)
    return block


def load_ids(sources, ids_vmem, ids_smem, sem):
    for i, src in enumerate(sources):
        ids = src[BODY:PAY, 0:128].astype(jnp.float32).astype(jnp.int32)
        ids_vmem[i] = ids[0:8, :]
    return pltpu.make_async_copy(ids_vmem, ids_smem, sem)


def scatter(src, ids, row, target, first):
    for m in range(RB):
        for s in range(SLOTS):
            block = m * SLOTS + s
            orbital = ids[row, 0, block]
            lanes = pl.ds(pl.multiple_of(orbital * AUX, AUX), AUX)
            rows = pl.ds(pl.multiple_of(first + m * BS, BS), BS)
            target[rows, lanes] = src[block * BS : (block + 1) * BS, :]


NT = (((1,), (1,)), ((), ()))


TYPES = 3
CHUNK = 2 * CHIP + 16
WIDE = CHIP + 16


def column_kernel(place_ref, *refs):
    column, (out_ref, ids_vmem, ids, sem) = refs[:4], refs[4:]
    copy = load_ids(column, ids_vmem, ids, sem)
    copy.start()
    out_ref[...] = jnp.zeros_like(out_ref)
    copy.wait()
    for i, d in enumerate((0, 2, 1, 3)):
        scatter(column[i], ids, i, out_ref, lax.rem(place_ref[0] + d, 4) * HALF)


def rows_kernel(src, out_ref, ids_vmem, ids, sem):
    halves = [src.at[k] for k in range(2)]
    copy = load_ids(halves, ids_vmem, ids, sem)
    copy.start()
    out_ref[...] = jnp.zeros_like(out_ref)
    copy.wait()
    for k in range(2):
        scatter(halves[k], ids, k, out_ref, k * HALF)


def pairs_kernel(place_ref, cols, own_rows, first_rows, src, out_ref, rows, ids_vmem, ids, sem):
    core = place_ref[1]
    rows_kernel(src, rows, ids_vmem, ids, sem)
    exponents = {}
    places = ((0, 0), (1 - core, core * CHIP), (core, (1 - core) * CHIP))
    for t, block in enumerate((own_rows, first_rows, rows)):
        part = lax.dot_general(block[...], cols[...], NT, preferred_element_type=jnp.float32)
        chunk, first = places[t]
        for i in range(4):
            coded, exponents[t, i] = encode(part[:, i * HALF : (i + 1) * HALF])
            at = pl.ds(first if t == 0 else pl.multiple_of(first, CHIP), CHIP)
            out_ref[i * 2 + chunk, at, :] = coded
    zero = core == 0
    for i in range(4):
        out_ref[i * 2 + 1, CHIP : 2 * CHIP, :] = jnp.zeros((CHIP, HALF), jnp.int16)
        near = jnp.where(zero, exponents[2, i], exponents[1, i])
        across = jnp.where(zero, exponents[1, i], exponents[2, i])
        out_ref[i * 2, 2 * CHIP :, :] = pick_rows([exponents[0, i], near], HALF).astype(jnp.int16)
        out_ref[i * 2 + 1, 2 * CHIP :, :] = pick_rows([across], HALF).astype(jnp.int16)


def middle_kernel(place_ref, in_ref, even_ref, odd_ref):
    tiles = []
    for u in range(2):
        halves = []
        for k in range(2):
            total = None
            for x in range(4):
                exps = in_ref[x * 2 + k, 2 * CHIP :, :].astype(jnp.int32)
                value = decode(in_ref[x * 2 + k, u * CHIP : (u + 1) * CHIP, :], exps, u)
                total = value if total is None else total + value
            halves.append(total)
        tiles.append(jnp.concatenate(halves, axis=1))
    first = encode(tiles[0])
    second = encode(jnp.where(place_ref[1] == 0, tiles[1], tiles[0].T))

    def write(ref, pair):
        ref[:CHIP, :] = pair[0]
        ref[CHIP:, :] = jnp.broadcast_to(pair[1], (16, CHIP)).astype(jnp.int16)

    even = lax.rem(place_ref[2], 2) == 0

    @pl.when(even)
    def _():
        write(even_ref, first)
        write(odd_ref, second)

    @pl.when(jnp.logical_not(even))
    def _():
        write(even_ref, second)
        write(odd_ref, first)


def join_kernel(place_ref, a_ref, b_ref, keep_ref, mirror_ref, send_ref):
    core = place_ref[1]
    for half, ref in ((core, mirror_ref), (1 - core, send_ref)):
        rows = pl.ds(pl.multiple_of(half * HALF, HALF), HALF)
        total = sum(
            decode(src[rows, :], src[CHIP:, :].astype(jnp.int32), 0) for src in (a_ref, b_ref)
        )
        if ref is mirror_ref:
            keep_ref[...] = total
        coded, exponent = encode(total)
        ref[:HALF, :] = coded
        ref[HALF:, :] = jnp.broadcast_to(exponent, (16, CHIP)).astype(jnp.int16)


def cross(z):
    return jnp.where(z < 2, 3 - z, z - 2)


def last_kernel(place_ref, keep_ref, mirror_ref, come_ref, out_ref):
    come = decode(come_ref[:HALF, :], come_ref[HALF:, :].astype(jnp.int32), 0)
    mirrored = place_ref[2] == cross(place_ref[3])

    @pl.when(mirrored)
    def _():
        kept = decode(mirror_ref[:HALF, :], mirror_ref[HALF:, :].astype(jnp.int32), 0)
        out_ref[...] = 0.25 * (kept + come)

    @pl.when(jnp.logical_not(mirrored))
    def _():
        out_ref[...] = 0.25 * (keep_ref[...] + come)


def index_of(x, zh, y, zl, c):
    return (((x * 4 + zh) * 4 + y) * 4 + zl) * 2 + c


def far_round(r):
    pairs = []
    for x in range(4):
        for s in range(4):
            for y in range(4):
                for z in range(4):
                    kinds = (
                        ((x, z, y, z), (x, z, y, z ^ 1)),
                        ((x, z, y, CROSS[z]), (x, CROSS[z], y, z)),
                    )
                    for c in range(2):
                        dest = kinds[c][(s + r) % 2]
                        pairs.append((index_of(x, s, y, z, c), index_of(*dest, s // 2)))
    return pairs


def home_round(swap_cores):
    pairs = []
    for x in range(4):
        for zh in range(4):
            for y in range(4):
                for z in range(4):
                    mirrored = zh == CROSS[z]
                    if not (mirrored or swap_cores):
                        continue
                    dest = (y, zh, x, z) if mirrored else (x, zh, y, z)
                    for c in range(2):
                        pairs.append((index_of(x, zh, y, z, c), index_of(*dest, c ^ swap_cores)))
    return pairs


def shards(raw_blocks, metric_factor, sig_list, live_count):
    place = jnp.stack([lax.axis_index("y"), lax.axis_index("c"), lax.axis_index("zh"), lax.axis_index("zl")])
    place = place.astype(jnp.int32)
    own = pl.pallas_call(
        contract_kernel,
        out_shape=jax.ShapeDtypeStruct((PAY, AUX), jnp.bfloat16),
        in_specs=[ANY, ANY, SMEM, SMEM],
        out_specs=VMEM,
        scratch_shapes=[
            pltpu.VMEM(raw_blocks.shape, jnp.bfloat16),
            pltpu.VMEM((AUX, AUX), jnp.bfloat16),
            pltpu.SemaphoreType.DMA((2,)),
        ],
        compiler_params=params(56),
        name="contract",
    )(raw_blocks, metric_factor, sig_list, live_count.reshape(RB))

    def swap(a):
        return lax.ppermute(a, "c", [(0, 1), (1, 0)])

    both = lax.all_gather(own, "c")
    along = lax.ppermute(
        both,
        ("zl", "c"),
        [(CROSS[i] * 2, i * 2) for i in range(4)] + [((i ^ 1) * 2 + 1, i * 2 + 1) for i in range(4)],
    )
    column = [own] + [lax.ppermute(own, "y", [((i + d) % 4, i) for i in range(4)]) for d in (2, 1, 3)]
    def ids_scratch(count):
        return [
            pltpu.VMEM((count, 8, 128), jnp.int32),
            pltpu.SMEM((count, 8, 128), jnp.int32),
            pltpu.SemaphoreType.DMA,
        ]

    def dense_rows(block):
        return pl.pallas_call(
            rows_kernel,
            out_shape=jax.ShapeDtypeStruct((CHIP, NOB * AUX), jnp.bfloat16),
            in_specs=[VMEM],
            out_specs=VMEM,
            scratch_shapes=ids_scratch(2),
            compiler_params=params(16),
            cost_estimate=pl.CostEstimate(flops=1_000_000_000, bytes_accessed=3_000_000, transcendentals=0),
            name="rows",
        )(block)

    dense = pl.pallas_call(
        column_kernel,
        out_shape=jax.ShapeDtypeStruct((4 * HALF, NOB * AUX), jnp.bfloat16),
        in_specs=[SMEM] + [VMEM] * 4,
        out_specs=VMEM,
        scratch_shapes=ids_scratch(4),
        compiler_params=params(16),
        cost_estimate=pl.CostEstimate(flops=20_000_000_000, bytes_accessed=6_000_000, transcendentals=0),
        name="column",
    )(place, *column)
    tiles = pl.pallas_call(
        pairs_kernel,
        out_shape=jax.ShapeDtypeStruct((8, CHUNK, HALF), jnp.int16),
        in_specs=[SMEM] + [VMEM] * 4,
        out_specs=VMEM,
        scratch_shapes=[pltpu.VMEM((CHIP, NOB * AUX), jnp.bfloat16)] + ids_scratch(2),
        compiler_params=params(16),
        name="pairs",
    )(place, dense, dense_rows(both), dense_rows(along), swap(along))
    arrived = lax.all_to_all(tiles, ("x", "c"), 0, 0, tiled=True)
    wide = jax.ShapeDtypeStruct((WIDE, CHIP), jnp.int16)
    messages = pl.pallas_call(
        middle_kernel,
        out_shape=[wide] * 2,
        in_specs=[SMEM, VMEM],
        out_specs=[VMEM] * 2,
        compiler_params=params(24),
        name="middle",
    )(place, arrived)
    half = jax.ShapeDtypeStruct((HALF, CHIP), jnp.float32)
    tile = jax.ShapeDtypeStruct((TILE, CHIP), jnp.int16)
    keep, mirror, send = pl.pallas_call(
        join_kernel,
        out_shape=[half, tile, tile],
        in_specs=[SMEM, VMEM, VMEM],
        out_specs=[VMEM] * 3,
        compiler_params=params(16),
        name="join",
    )(place, *[lax.ppermute(a, AXES, far_round(r)) for r, a in enumerate(messages)])
    return pl.pallas_call(
        last_kernel,
        out_shape=half,
        in_specs=[SMEM] + [VMEM] * 3,
        out_specs=VMEM,
        compiler_params=params(16),
        name="last",
    )(place, keep, lax.ppermute(mirror, AXES, home_round(0)), lax.ppermute(send, AXES, home_round(1)))


def solution(mesh):
    fine = Mesh(mesh.devices.reshape(4, 4, 4, 4, 2), AXES)
    blk, grp = ("y", "zl", "c"), ("x", "zh")
    placed = (P(blk, grp, None, None), P(), P(blk, grp), P(blk, grp))
    return jax.shard_map(shards, mesh=fine, in_specs=placed, out_specs=P(blk, grp), check_vma=False)
```

```python
import jax
import jax.numpy as jnp
from jax import lax
from jax.experimental import pallas as pl
from jax.experimental.pallas import tpu as pltpu
from jax.sharding import Mesh, PartitionSpec as P

AXES = ("x", "zh", "y", "zl", "c")
NOB = 16
SLOTS = 6
BS = 64
AUX = 256
RB = 2
HALF = RB * BS
CHIP = 2 * HALF
BODY = RB * SLOTS * BS
PAY = BODY + 16
TILE = HALF + 16
LEVELS = 32000.0
CROSS = (3, 2, 0, 1)
VMEM = pl.BlockSpec(memory_space=pltpu.VMEM)
SMEM = pl.BlockSpec(memory_space=pltpu.SMEM)
ANY = pl.BlockSpec(memory_space=pl.ANY)


def params(mib):
    return pltpu.CompilerParams(vmem_limit_bytes=mib * 1024 * 1024)


def contract_kernel(raw_hbm, metric_hbm, sig_ref, live_ref, out_ref, raw_ref, metric_ref, sems):
    copies = [
        pltpu.make_async_copy(metric_hbm, metric_ref, sems.at[0]),
        pltpu.make_async_copy(raw_hbm, raw_ref, sems.at[1]),
    ]
    for copy in copies:
        copy.start()
    lane = lax.broadcasted_iota(jnp.int32, (16, AUX), 1)
    ids = jnp.zeros((16, AUX), jnp.int32)
    for m in range(RB):
        for s in range(SLOTS):
            ids = jnp.where(lane == m * SLOTS + s, sig_ref[m, s], ids)
    out_ref[BODY:, :] = ids.astype(jnp.float32).astype(jnp.bfloat16)
    for copy in copies:
        copy.wait()
    for m in range(RB):
        for s in range(SLOTS):
            block = m * SLOTS + s
            product = jnp.dot(
                raw_ref[m, s], metric_ref[...], preferred_element_type=jnp.float32
            )
            live = (s < live_ref[m]).astype(jnp.float32)
            out_ref[block * BS : (block + 1) * BS, :] = (product * live).astype(jnp.bfloat16)


def encode(values):
    top = jnp.max(jnp.abs(values), axis=0, keepdims=True)
    exponent = jnp.ceil(jnp.log2(jnp.maximum(top, 1e-30)) + 1e-3)
    coded = jnp.round(values * (LEVELS * jnp.exp2(-exponent)))
    return coded.astype(jnp.int32).astype(jnp.int16), exponent.astype(jnp.int32)


def decode(coded, exponents, row):
    scale = jnp.exp2(exponents[row : row + 1, :].astype(jnp.float32)) * (1.0 / LEVELS)
    return coded.astype(jnp.int32).astype(jnp.float32) * scale


def pick_rows(rows, width):
    at = lax.broadcasted_iota(jnp.int32, (16, width), 0)
    block = jnp.zeros((16, width), jnp.int32)
    for i, row in enumerate(rows):
        block = jnp.where(at == i, jnp.broadcast_to(row, (16, width)), block)
    return block


def load_ids(sources, ids_vmem, ids_smem, sem):
    for i, src in enumerate(sources):
        ids = src[BODY:PAY, 0:128].astype(jnp.float32).astype(jnp.int32)
        ids_vmem[i] = ids[0:8, :]
    return pltpu.make_async_copy(ids_vmem, ids_smem, sem)


def scatter(src, ids, row, target, first):
    for m in range(RB):
        for s in range(SLOTS):
            block = m * SLOTS + s
            orbital = ids[row, 0, block]
            lanes = pl.ds(pl.multiple_of(orbital * AUX, AUX), AUX)
            rows = pl.ds(pl.multiple_of(first + m * BS, BS), BS)
            target[rows, lanes] = src[block * BS : (block + 1) * BS, :]


NT = (((1,), (1,)), ((), ()))


TYPES = 3
CHUNK = 2 * CHIP + 16
WIDE = CHIP + 16


def column_kernel(place_ref, *refs):
    column, (out_ref, ids_vmem, ids, sem) = refs[:4], refs[4:]
    copy = load_ids(column, ids_vmem, ids, sem)
    copy.start()
    out_ref[...] = jnp.zeros_like(out_ref)
    copy.wait()
    for i, d in enumerate((0, 2, 1, 3)):
        scatter(column[i], ids, i, out_ref, lax.rem(place_ref[0] + d, 4) * HALF)


def rows_kernel(place_ref, mine, other, out_ref, ids_vmem, ids, sem):
    core = place_ref[1]
    copy = load_ids([mine, other], ids_vmem, ids, sem)
    copy.start()
    out_ref[...] = jnp.zeros_like(out_ref)
    copy.wait()
    scatter(mine, ids, 0, out_ref, core * HALF)
    scatter(other, ids, 1, out_ref, (1 - core) * HALF)


def pairs_kernel(cols, own_rows, across_rows, near_rows, out_ref):
    exponents = {}
    for t, block in enumerate((own_rows, near_rows, across_rows)):
        part = lax.dot_general(block[...], cols[...], NT, preferred_element_type=jnp.float32)
        for i in range(4):
            coded, exponents[t, i] = encode(part[:, i * HALF : (i + 1) * HALF])
            first = (t % 2) * CHIP
            out_ref[i * 2 + t // 2, first : first + CHIP, :] = coded
    for i in range(4):
        out_ref[i * 2 + 1, CHIP : 2 * CHIP, :] = jnp.zeros((CHIP, HALF), jnp.int16)
        for k in range(2):
            block = pick_rows([exponents[k * 2, i], exponents[1, i]], HALF)
            out_ref[i * 2 + k, 2 * CHIP :, :] = block.astype(jnp.int16)


def middle_kernel(place_ref, in_ref, even_ref, odd_ref):
    tiles = []
    for u in range(2):
        halves = []
        for k in range(2):
            total = None
            for x in range(4):
                exps = in_ref[x * 2 + k, 2 * CHIP :, :].astype(jnp.int32)
                value = decode(in_ref[x * 2 + k, u * CHIP : (u + 1) * CHIP, :], exps, u)
                total = value if total is None else total + value
            halves.append(total)
        tiles.append(jnp.concatenate(halves, axis=1))
    first = encode(tiles[0])
    second = encode(jnp.where(place_ref[1] == 0, tiles[1], tiles[0].T))

    def write(ref, pair):
        ref[:CHIP, :] = pair[0]
        ref[CHIP:, :] = jnp.broadcast_to(pair[1], (16, CHIP)).astype(jnp.int16)

    even = lax.rem(place_ref[2], 2) == 0

    @pl.when(even)
    def _():
        write(even_ref, first)
        write(odd_ref, second)

    @pl.when(jnp.logical_not(even))
    def _():
        write(even_ref, second)
        write(odd_ref, first)


def join_kernel(place_ref, a_ref, b_ref, keep_ref, send_ref):
    core = place_ref[1]
    for ref, half in ((keep_ref, core), (send_ref, 1 - core)):
        rows = pl.ds(pl.multiple_of(half * HALF, HALF), HALF)
        ref[...] = sum(
            decode(src[rows, :], src[CHIP:, :].astype(jnp.int32), 0) for src in (a_ref, b_ref)
        )


def last_kernel(keep_ref, come_ref, out_ref):
    out_ref[...] = 0.25 * (keep_ref[...] + come_ref[...])


def index_of(x, zh, y, zl, c):
    return (((x * 4 + zh) * 4 + y) * 4 + zl) * 2 + c


def far_round(r):
    pairs = []
    for x in range(4):
        for s in range(4):
            for y in range(4):
                for z in range(4):
                    kinds = (
                        ((x, z, y, z), (x, z, y, z ^ 1)),
                        ((x, z, y, CROSS[z]), (y, CROSS[z], x, z)),
                    )
                    for c in range(2):
                        dest = kinds[c][(s + r) % 2]
                        pairs.append((index_of(x, s, y, z, c), index_of(*dest, s // 2)))
    return pairs


def shards(raw_blocks, metric_factor, sig_list, live_count):
    place = jnp.stack([lax.axis_index("y"), lax.axis_index("c"), lax.axis_index("zh")]).astype(jnp.int32)
    own = pl.pallas_call(
        contract_kernel,
        out_shape=jax.ShapeDtypeStruct((PAY, AUX), jnp.bfloat16),
        in_specs=[ANY, ANY, SMEM, SMEM],
        out_specs=VMEM,
        scratch_shapes=[
            pltpu.VMEM(raw_blocks.shape, jnp.bfloat16),
            pltpu.VMEM((AUX, AUX), jnp.bfloat16),
            pltpu.SemaphoreType.DMA((2,)),
        ],
        compiler_params=params(56),
        name="contract",
    )(raw_blocks, metric_factor, sig_list, live_count.reshape(RB))

    def swap(a):
        return lax.ppermute(a, "c", [(0, 1), (1, 0)])

    across = lax.ppermute(own, "zl", [(CROSS[i], i) for i in range(4)])
    near = lax.ppermute(own, "zl", [(i ^ 1, i) for i in range(4)])
    column = [own] + [lax.ppermute(own, "y", [((i + d) % 4, i) for i in range(4)]) for d in (2, 1, 3)]
    def ids_scratch(count):
        return [
            pltpu.VMEM((count, 8, 128), jnp.int32),
            pltpu.SMEM((count, 8, 128), jnp.int32),
            pltpu.SemaphoreType.DMA,
        ]

    def dense_rows(block, flops):
        return pl.pallas_call(
            rows_kernel,
            out_shape=jax.ShapeDtypeStruct((CHIP, NOB * AUX), jnp.bfloat16),
            in_specs=[SMEM, VMEM, VMEM],
            out_specs=VMEM,
            scratch_shapes=ids_scratch(2),
            compiler_params=params(16),
            cost_estimate=pl.CostEstimate(flops=flops, bytes_accessed=3_000_000, transcendentals=0),
            name="rows",
        )(place, block, swap(block))

    dense = pl.pallas_call(
        column_kernel,
        out_shape=jax.ShapeDtypeStruct((4 * HALF, NOB * AUX), jnp.bfloat16),
        in_specs=[SMEM] + [VMEM] * 4,
        out_specs=VMEM,
        scratch_shapes=ids_scratch(4),
        compiler_params=params(16),
        cost_estimate=pl.CostEstimate(flops=12_000_000_000, bytes_accessed=6_000_000, transcendentals=0),
        name="column",
    )(place, *column)
    tiles = pl.pallas_call(
        pairs_kernel,
        out_shape=jax.ShapeDtypeStruct((8, CHUNK, HALF), jnp.int16),
        in_specs=[VMEM] * 4,
        out_specs=VMEM,
        compiler_params=params(24),
        name="pairs",
    )(
        dense,
        dense_rows(own, 1_000_000_000),
        dense_rows(across, 1_000_000_000),
        dense_rows(near, 1_000_000_000),
    )
    arrived = lax.all_to_all(tiles, ("x", "c"), 0, 0, tiled=True)
    wide = jax.ShapeDtypeStruct((WIDE, CHIP), jnp.int16)
    messages = pl.pallas_call(
        middle_kernel,
        out_shape=[wide] * 2,
        in_specs=[SMEM, VMEM],
        out_specs=[VMEM] * 2,
        compiler_params=params(24),
        name="middle",
    )(place, arrived)
    half = jax.ShapeDtypeStruct((HALF, CHIP), jnp.float32)
    keep, send = pl.pallas_call(
        join_kernel,
        out_shape=[half] * 2,
        in_specs=[SMEM, VMEM, VMEM],
        out_specs=[VMEM] * 2,
        compiler_params=params(16),
        name="join",
    )(place, *[lax.ppermute(a, AXES, far_round(r)) for r, a in enumerate(messages)])
    return pl.pallas_call(
        last_kernel,
        out_shape=half,
        in_specs=[VMEM] * 2,
        out_specs=VMEM,
        compiler_params=params(16),
        name="last",
    )(keep, swap(send))


def solution(mesh):
    fine = Mesh(mesh.devices.reshape(4, 4, 4, 4, 2), AXES)
    blk, grp = ("y", "zl", "c"), ("x", "zh")
    placed = (P(blk, grp, None, None), P(), P(blk, grp), P(blk, grp))
    return jax.shard_map(shards, mesh=fine, in_specs=placed, out_specs=P(blk, grp), check_vma=False)
```

```python
import jax
import jax.numpy as jnp
from jax import lax
from jax.experimental import pallas as pl
from jax.experimental.pallas import tpu as pltpu
from jax.sharding import Mesh, PartitionSpec as P

AXES = ("x", "zh", "y", "zl", "c")
NOB = 16
SLOTS = 6
BS = 64
AUX = 256
RB = 2
HALF = RB * BS
CHIP = 2 * HALF
BODY = RB * SLOTS * BS
PAY = BODY + 16
TILE = HALF + 16
LEVELS = 32000.0
CROSS = (3, 2, 0, 1)
VMEM = pl.BlockSpec(memory_space=pltpu.VMEM)
SMEM = pl.BlockSpec(memory_space=pltpu.SMEM)
ANY = pl.BlockSpec(memory_space=pl.ANY)


def params(mib):
    return pltpu.CompilerParams(vmem_limit_bytes=mib * 1024 * 1024)


def contract_kernel(raw_hbm, metric_hbm, sig_ref, live_ref, out_ref, raw_ref, metric_ref, sems):
    copies = [
        pltpu.make_async_copy(metric_hbm, metric_ref, sems.at[0]),
        pltpu.make_async_copy(raw_hbm, raw_ref, sems.at[1]),
    ]
    for copy in copies:
        copy.start()
    lane = lax.broadcasted_iota(jnp.int32, (16, AUX), 1)
    ids = jnp.zeros((16, AUX), jnp.int32)
    for m in range(RB):
        for s in range(SLOTS):
            ids = jnp.where(lane == m * SLOTS + s, sig_ref[m, s], ids)
    out_ref[BODY:, :] = ids.astype(jnp.float32).astype(jnp.bfloat16)
    for copy in copies:
        copy.wait()
    for m in range(RB):
        for s in range(SLOTS):
            block = m * SLOTS + s
            product = jnp.dot(
                raw_ref[m, s], metric_ref[...], preferred_element_type=jnp.float32
            )
            live = (s < live_ref[m]).astype(jnp.float32)
            out_ref[block * BS : (block + 1) * BS, :] = (product * live).astype(jnp.bfloat16)


def encode(values):
    top = jnp.max(jnp.abs(values), axis=0, keepdims=True)
    exponent = jnp.ceil(jnp.log2(jnp.maximum(top, 1e-30)) + 1e-3)
    coded = jnp.round(values * (LEVELS * jnp.exp2(-exponent)))
    return coded.astype(jnp.int32).astype(jnp.int16), exponent.astype(jnp.int32)


def decode(coded, exponents, row):
    scale = jnp.exp2(exponents[row : row + 1, :].astype(jnp.float32)) * (1.0 / LEVELS)
    return coded.astype(jnp.int32).astype(jnp.float32) * scale


def pick_rows(rows, width):
    at = lax.broadcasted_iota(jnp.int32, (16, width), 0)
    block = jnp.zeros((16, width), jnp.int32)
    for i, row in enumerate(rows):
        block = jnp.where(at == i, jnp.broadcast_to(row, (16, width)), block)
    return block


def load_ids(sources, ids_vmem, ids_smem, sem):
    for i, src in enumerate(sources):
        ids = src[BODY:PAY, 0:128].astype(jnp.float32).astype(jnp.int32)
        ids_vmem[i] = ids[0:8, :]
    return pltpu.make_async_copy(ids_vmem, ids_smem, sem)


def scatter(src, ids, row, target, first):
    for m in range(RB):
        for s in range(SLOTS):
            block = m * SLOTS + s
            orbital = ids[row, 0, block]
            lanes = pl.ds(pl.multiple_of(orbital * AUX, AUX), AUX)
            rows = pl.ds(pl.multiple_of(first + m * BS, BS), BS)
            target[rows, lanes] = src[block * BS : (block + 1) * BS, :]


NT = (((1,), (1,)), ((), ()))


TYPES = 3
CHUNK = 2 * CHIP + 16
WIDE = CHIP + 16


def column_kernel(place_ref, *refs):
    column, (out_ref, ids_vmem, ids, sem) = refs[:4], refs[4:]
    copy = load_ids(column, ids_vmem, ids, sem)
    copy.start()
    out_ref[...] = jnp.zeros_like(out_ref)
    copy.wait()
    for i, d in enumerate((0, 2, 1, 3)):
        scatter(column[i], ids, i, out_ref, lax.rem(place_ref[0] + d, 4) * HALF)


def rows_kernel(src, out_ref, ids_vmem, ids, sem):
    halves = [src.at[k] for k in range(2)]
    copy = load_ids(halves, ids_vmem, ids, sem)
    copy.start()
    out_ref[...] = jnp.zeros_like(out_ref)
    copy.wait()
    for k in range(2):
        scatter(halves[k], ids, k, out_ref, k * HALF)


def pairs_kernel(place_ref, cols, own_rows, first_rows, src, out_ref, rows, ids_vmem, ids, sem):
    core = place_ref[1]
    rows_kernel(src, rows, ids_vmem, ids, sem)
    exponents = {}
    places = ((0, 0), (1 - core, core * CHIP), (core, (1 - core) * CHIP))
    for t, block in enumerate((own_rows, first_rows, rows)):
        part = lax.dot_general(block[...], cols[...], NT, preferred_element_type=jnp.float32)
        chunk, first = places[t]
        for i in range(4):
            coded, exponents[t, i] = encode(part[:, i * HALF : (i + 1) * HALF])
            at = pl.ds(first if t == 0 else pl.multiple_of(first, CHIP), CHIP)
            out_ref[i * 2 + chunk, at, :] = coded
    zero = core == 0
    for i in range(4):
        out_ref[i * 2 + 1, CHIP : 2 * CHIP, :] = jnp.zeros((CHIP, HALF), jnp.int16)
        near = jnp.where(zero, exponents[2, i], exponents[1, i])
        across = jnp.where(zero, exponents[1, i], exponents[2, i])
        out_ref[i * 2, 2 * CHIP :, :] = pick_rows([exponents[0, i], near], HALF).astype(jnp.int16)
        out_ref[i * 2 + 1, 2 * CHIP :, :] = pick_rows([across], HALF).astype(jnp.int16)


def middle_kernel(place_ref, in_ref, first_ref, second_ref):
    tiles = []
    for u in range(2):
        halves = []
        for k in range(2):
            total = None
            for x in range(4):
                exps = in_ref[x * 2 + k, 2 * CHIP :, :].astype(jnp.int32)
                value = decode(in_ref[x * 2 + k, u * CHIP : (u + 1) * CHIP, :], exps, u)
                total = value if total is None else total + value
            halves.append(total)
        tiles.append(jnp.concatenate(halves, axis=1))
    first = encode(tiles[0])
    second = encode(jnp.where(place_ref[1] == 0, tiles[1], tiles[0].T))

    def write(ref, pair):
        ref[:CHIP, :] = pair[0]
        ref[CHIP:, :] = jnp.broadcast_to(pair[1], (16, CHIP)).astype(jnp.int16)

    z = place_ref[3]
    to = jnp.where(place_ref[1] == 0, z, jnp.where(z < 2, 3 - z, z - 2))
    far = lax.rem(place_ref[2] + 4 - to, 4) >= 2
    straight = jnp.logical_xor(far, place_ref[1] == 1)

    @pl.when(straight)
    def _():
        write(first_ref, first)
        write(second_ref, second)

    @pl.when(jnp.logical_not(straight))
    def _():
        write(first_ref, second)
        write(second_ref, first)


def join_kernel(place_ref, a_ref, b_ref, keep_ref, send_ref):
    core = place_ref[1]
    for ref, half in ((keep_ref, core), (send_ref, 1 - core)):
        rows = pl.ds(pl.multiple_of(half * HALF, HALF), HALF)
        ref[...] = sum(
            decode(src[rows, :], src[CHIP:, :].astype(jnp.int32), 0) for src in (a_ref, b_ref)
        )


def last_kernel(keep_ref, come_ref, out_ref):
    out_ref[...] = 0.25 * (keep_ref[...] + come_ref[...])


def index_of(x, zh, y, zl, c):
    return (((x * 4 + zh) * 4 + y) * 4 + zl) * 2 + c


def far_round(r):
    pairs = []
    for x in range(4):
        for s in range(4):
            for y in range(4):
                for z in range(4):
                    kinds = (
                        ((x, z, y, z), (x, z, y, z ^ 1)),
                        ((x, z, y, CROSS[z]), (y, CROSS[z], x, z)),
                    )
                    for c in range(2):
                        away = (s - (CROSS[z] if c else z)) % 4
                        straight = (away >= 2) != (c == 1)
                        dest = kinds[c][r if straight else 1 - r]
                        pairs.append((index_of(x, s, y, z, c), index_of(*dest, away % 2)))
    return pairs


def shards(raw_blocks, metric_factor, sig_list, live_count):
    place = jnp.stack([lax.axis_index("y"), lax.axis_index("c"), lax.axis_index("zh"), lax.axis_index("zl")])
    place = place.astype(jnp.int32)
    own = pl.pallas_call(
        contract_kernel,
        out_shape=jax.ShapeDtypeStruct((PAY, AUX), jnp.bfloat16),
        in_specs=[ANY, ANY, SMEM, SMEM],
        out_specs=VMEM,
        scratch_shapes=[
            pltpu.VMEM(raw_blocks.shape, jnp.bfloat16),
            pltpu.VMEM((AUX, AUX), jnp.bfloat16),
            pltpu.SemaphoreType.DMA((2,)),
        ],
        compiler_params=params(56),
        name="contract",
    )(raw_blocks, metric_factor, sig_list, live_count.reshape(RB))

    def swap(a):
        return lax.ppermute(a, "c", [(0, 1), (1, 0)])

    both = lax.all_gather(own, "c")
    along = lax.ppermute(
        both,
        ("zl", "c"),
        [(CROSS[i] * 2, i * 2) for i in range(4)] + [((i ^ 1) * 2 + 1, i * 2 + 1) for i in range(4)],
    )
    column = [own] + [lax.ppermute(own, "y", [((i + d) % 4, i) for i in range(4)]) for d in (2, 1, 3)]
    def ids_scratch(count):
        return [
            pltpu.VMEM((count, 8, 128), jnp.int32),
            pltpu.SMEM((count, 8, 128), jnp.int32),
            pltpu.SemaphoreType.DMA,
        ]

    def dense_rows(block):
        return pl.pallas_call(
            rows_kernel,
            out_shape=jax.ShapeDtypeStruct((CHIP, NOB * AUX), jnp.bfloat16),
            in_specs=[VMEM],
            out_specs=VMEM,
            scratch_shapes=ids_scratch(2),
            compiler_params=params(16),
            cost_estimate=pl.CostEstimate(flops=1_000_000_000, bytes_accessed=3_000_000, transcendentals=0),
            name="rows",
        )(block)

    dense = pl.pallas_call(
        column_kernel,
        out_shape=jax.ShapeDtypeStruct((4 * HALF, NOB * AUX), jnp.bfloat16),
        in_specs=[SMEM] + [VMEM] * 4,
        out_specs=VMEM,
        scratch_shapes=ids_scratch(4),
        compiler_params=params(16),
        cost_estimate=pl.CostEstimate(flops=20_000_000_000, bytes_accessed=6_000_000, transcendentals=0),
        name="column",
    )(place, *column)
    tiles = pl.pallas_call(
        pairs_kernel,
        out_shape=jax.ShapeDtypeStruct((8, CHUNK, HALF), jnp.int16),
        in_specs=[SMEM] + [VMEM] * 4,
        out_specs=VMEM,
        scratch_shapes=[pltpu.VMEM((CHIP, NOB * AUX), jnp.bfloat16)] + ids_scratch(2),
        compiler_params=params(16),
        name="pairs",
    )(place, dense, dense_rows(both), dense_rows(along), swap(along))
    arrived = lax.all_to_all(tiles, ("x", "c"), 0, 0, tiled=True)
    wide = jax.ShapeDtypeStruct((WIDE, CHIP), jnp.int16)
    messages = pl.pallas_call(
        middle_kernel,
        out_shape=[wide] * 2,
        in_specs=[SMEM, VMEM],
        out_specs=[VMEM] * 2,
        compiler_params=params(24),
        name="middle",
    )(place, arrived)
    half = jax.ShapeDtypeStruct((HALF, CHIP), jnp.float32)
    keep, send = pl.pallas_call(
        join_kernel,
        out_shape=[half] * 2,
        in_specs=[SMEM, VMEM, VMEM],
        out_specs=[VMEM] * 2,
        compiler_params=params(16),
        name="join",
    )(place, *[lax.ppermute(a, AXES, far_round(r)) for r, a in enumerate(messages)])
    return pl.pallas_call(
        last_kernel,
        out_shape=half,
        in_specs=[VMEM] * 2,
        out_specs=VMEM,
        compiler_params=params(16),
        name="last",
    )(keep, swap(send))


def solution(mesh):
    fine = Mesh(mesh.devices.reshape(4, 4, 4, 4, 2), AXES)
    blk, grp = ("y", "zl", "c"), ("x", "zh")
    placed = (P(blk, grp, None, None), P(), P(blk, grp), P(blk, grp))
    return jax.shard_map(shards, mesh=fine, in_specs=placed, out_specs=P(blk, grp), check_vma=False)
```

```python
import jax
import jax.numpy as jnp
from jax import lax
from jax.experimental import pallas as pl
from jax.experimental.pallas import tpu as pltpu
from jax.sharding import Mesh, PartitionSpec as P

AXES = ("x", "zh", "y", "zl", "c")
NOB = 16
SLOTS = 6
BS = 64
AUX = 256
RB = 2
HALF = RB * BS
CHIP = 2 * HALF
BODY = RB * SLOTS * BS
PAY = BODY + 16
TILE = HALF + 16
LEVELS = 32000.0
CROSS = (3, 2, 0, 1)
VMEM = pl.BlockSpec(memory_space=pltpu.VMEM)
SMEM = pl.BlockSpec(memory_space=pltpu.SMEM)
ANY = pl.BlockSpec(memory_space=pl.ANY)


def params(mib):
    return pltpu.CompilerParams(vmem_limit_bytes=mib * 1024 * 1024)


def contract_kernel(raw_hbm, metric_hbm, sig_ref, live_ref, out_ref, raw_ref, metric_ref, sems):
    copies = [
        pltpu.make_async_copy(metric_hbm, metric_ref, sems.at[0]),
        pltpu.make_async_copy(raw_hbm, raw_ref, sems.at[1]),
    ]
    for copy in copies:
        copy.start()
    lane = lax.broadcasted_iota(jnp.int32, (16, AUX), 1)
    ids = jnp.zeros((16, AUX), jnp.int32)
    for m in range(RB):
        for s in range(SLOTS):
            ids = jnp.where(lane == m * SLOTS + s, sig_ref[m, s], ids)
    out_ref[BODY:, :] = ids.astype(jnp.float32).astype(jnp.bfloat16)
    for copy in copies:
        copy.wait()
    for m in range(RB):
        for s in range(SLOTS):
            block = m * SLOTS + s
            product = jnp.dot(
                raw_ref[m, s], metric_ref[...], preferred_element_type=jnp.float32
            )
            live = (s < live_ref[m]).astype(jnp.float32)
            out_ref[block * BS : (block + 1) * BS, :] = (product * live).astype(jnp.bfloat16)


def encode(values):
    top = jnp.max(jnp.abs(values), axis=0, keepdims=True)
    exponent = jnp.ceil(jnp.log2(jnp.maximum(top, 1e-30)) + 1e-3)
    coded = jnp.round(values * (LEVELS * jnp.exp2(-exponent)))
    return coded.astype(jnp.int32).astype(jnp.int16), exponent.astype(jnp.int32)


def decode(coded, exponents, row):
    scale = jnp.exp2(exponents[row : row + 1, :].astype(jnp.float32)) * (1.0 / LEVELS)
    return coded.astype(jnp.int32).astype(jnp.float32) * scale


def pick_rows(rows, width):
    at = lax.broadcasted_iota(jnp.int32, (16, width), 0)
    block = jnp.zeros((16, width), jnp.int32)
    for i, row in enumerate(rows):
        block = jnp.where(at == i, jnp.broadcast_to(row, (16, width)), block)
    return block


def load_ids(sources, ids_vmem, ids_smem, sem):
    for i, src in enumerate(sources):
        ids = src[BODY:PAY, 0:128].astype(jnp.float32).astype(jnp.int32)
        ids_vmem[i] = ids[0:8, :]
    return pltpu.make_async_copy(ids_vmem, ids_smem, sem)


def scatter(src, ids, row, target, first):
    for m in range(RB):
        for s in range(SLOTS):
            block = m * SLOTS + s
            orbital = ids[row, 0, block]
            lanes = pl.ds(pl.multiple_of(orbital * AUX, AUX), AUX)
            rows = pl.ds(pl.multiple_of(first + m * BS, BS), BS)
            target[rows, lanes] = src[block * BS : (block + 1) * BS, :]


NT = (((1,), (1,)), ((), ()))


TYPES = 3
CHUNK = 2 * CHIP + 16
WIDE = CHIP + 16


def column_kernel(place_ref, *refs):
    column, (out_ref, ids_vmem, ids, sem) = refs[:4], refs[5:]
    copy = load_ids(column, ids_vmem, ids, sem)
    copy.start()
    out_ref[...] = jnp.zeros_like(out_ref)
    copy.wait()
    for i, d in enumerate((0, 2, 1, 3)):
        scatter(column[i], ids, i, out_ref, lax.rem(place_ref[0] + d, 4) * HALF)


def rows_kernel(src, out_ref, ids_vmem, ids, sem):
    halves = [src.at[k] for k in range(2)]
    copy = load_ids(halves, ids_vmem, ids, sem)
    copy.start()
    out_ref[...] = jnp.zeros_like(out_ref)
    copy.wait()
    for k in range(2):
        scatter(halves[k], ids, k, out_ref, k * HALF)


def pairs_kernel(place_ref, cols, own_rows, first_rows, src, out_ref, rows, ids_vmem, ids, sem):
    core = place_ref[1]
    rows_kernel(src, rows, ids_vmem, ids, sem)
    exponents = {}
    places = ((0, 0), (1 - core, core * CHIP), (core, (1 - core) * CHIP))
    for t, block in enumerate((own_rows, first_rows, rows)):
        part = lax.dot_general(block[...], cols[...], NT, preferred_element_type=jnp.float32)
        chunk, first = places[t]
        for i in range(4):
            coded, exponents[t, i] = encode(part[:, i * HALF : (i + 1) * HALF])
            at = pl.ds(first if t == 0 else pl.multiple_of(first, CHIP), CHIP)
            out_ref[i * 2 + chunk, at, :] = coded
    zero = core == 0
    for i in range(4):
        out_ref[i * 2 + 1, CHIP : 2 * CHIP, :] = jnp.zeros((CHIP, HALF), jnp.int16)
        near = jnp.where(zero, exponents[2, i], exponents[1, i])
        across = jnp.where(zero, exponents[1, i], exponents[2, i])
        out_ref[i * 2, 2 * CHIP :, :] = pick_rows([exponents[0, i], near], HALF).astype(jnp.int16)
        out_ref[i * 2 + 1, 2 * CHIP :, :] = pick_rows([across], HALF).astype(jnp.int16)


def middle_kernel(place_ref, in_ref, first_ref, second_ref):
    tiles = []
    for u in range(2):
        halves = []
        for k in range(2):
            total = None
            for x in range(4):
                exps = in_ref[x * 2 + k, 2 * CHIP :, :].astype(jnp.int32)
                value = decode(in_ref[x * 2 + k, u * CHIP : (u + 1) * CHIP, :], exps, u)
                total = value if total is None else total + value
            halves.append(total)
        tiles.append(jnp.concatenate(halves, axis=1))
    first = encode(tiles[0])
    second = encode(jnp.where(place_ref[1] == 0, tiles[1], tiles[0].T))

    def write(ref, pair):
        ref[:CHIP, :] = pair[0]
        ref[CHIP:, :] = jnp.broadcast_to(pair[1], (16, CHIP)).astype(jnp.int16)

    z = place_ref[3]
    to = jnp.where(place_ref[1] == 0, z, jnp.where(z < 2, 3 - z, z - 2))
    far = lax.rem(place_ref[2] + 4 - to, 4) >= 2
    straight = jnp.logical_xor(far, place_ref[1] == 1)

    @pl.when(straight)
    def _():
        write(first_ref, first)
        write(second_ref, second)

    @pl.when(jnp.logical_not(straight))
    def _():
        write(first_ref, second)
        write(second_ref, first)


def join_kernel(place_ref, a_ref, b_ref, keep_ref, send_ref):
    core = place_ref[1]
    for ref, half in ((keep_ref, core), (send_ref, 1 - core)):
        rows = pl.ds(pl.multiple_of(half * HALF, HALF), HALF)
        ref[...] = sum(
            decode(src[rows, :], src[CHIP:, :].astype(jnp.int32), 0) for src in (a_ref, b_ref)
        )


def last_kernel(keep_ref, come_ref, out_ref):
    out_ref[...] = 0.25 * (keep_ref[...] + come_ref[...])


def index_of(x, zh, y, zl, c):
    return (((x * 4 + zh) * 4 + y) * 4 + zl) * 2 + c


def far_round(r):
    pairs = []
    for x in range(4):
        for s in range(4):
            for y in range(4):
                for z in range(4):
                    kinds = (
                        ((x, z, y, z), (x, z, y, z ^ 1)),
                        ((x, z, y, CROSS[z]), (y, CROSS[z], x, z)),
                    )
                    for c in range(2):
                        away = (s - (CROSS[z] if c else z)) % 4
                        straight = (away >= 2) != (c == 1)
                        dest = kinds[c][r if straight else 1 - r]
                        pairs.append((index_of(x, s, y, z, c), index_of(*dest, away % 2)))
    return pairs


def shards(raw_blocks, metric_factor, sig_list, live_count):
    place = jnp.stack([lax.axis_index("y"), lax.axis_index("c"), lax.axis_index("zh"), lax.axis_index("zl")])
    place = place.astype(jnp.int32)
    own = pl.pallas_call(
        contract_kernel,
        out_shape=jax.ShapeDtypeStruct((PAY, AUX), jnp.bfloat16),
        in_specs=[ANY, ANY, SMEM, SMEM],
        out_specs=VMEM,
        scratch_shapes=[
            pltpu.VMEM(raw_blocks.shape, jnp.bfloat16),
            pltpu.VMEM((AUX, AUX), jnp.bfloat16),
            pltpu.SemaphoreType.DMA((2,)),
        ],
        compiler_params=params(56),
        name="contract",
    )(raw_blocks, metric_factor, sig_list, live_count.reshape(RB))

    def swap(a):
        return lax.ppermute(a, "c", [(0, 1), (1, 0)])

    both = lax.all_gather(own, "c")
    along = lax.ppermute(
        both,
        ("zl", "c"),
        [(CROSS[i] * 2, i * 2) for i in range(4)] + [((i ^ 1) * 2 + 1, i * 2 + 1) for i in range(4)],
    )
    column = [own] + [lax.ppermute(own, "y", [((i + d) % 4, i) for i in range(4)]) for d in (2, 1, 3)]
    def ids_scratch(count):
        return [
            pltpu.VMEM((count, 8, 128), jnp.int32),
            pltpu.SMEM((count, 8, 128), jnp.int32),
            pltpu.SemaphoreType.DMA,
        ]

    def dense_rows(block):
        return pl.pallas_call(
            rows_kernel,
            out_shape=jax.ShapeDtypeStruct((CHIP, NOB * AUX), jnp.bfloat16),
            in_specs=[VMEM],
            out_specs=VMEM,
            scratch_shapes=ids_scratch(2),
            compiler_params=params(16),
            cost_estimate=pl.CostEstimate(flops=1_000_000_000, bytes_accessed=3_000_000, transcendentals=0),
            name="rows",
        )(block)

    first_rows = dense_rows(along)
    dense = pl.pallas_call(
        column_kernel,
        out_shape=jax.ShapeDtypeStruct((4 * HALF, NOB * AUX), jnp.bfloat16),
        in_specs=[SMEM] + [VMEM] * 4 + [ANY],
        out_specs=VMEM,
        scratch_shapes=ids_scratch(4),
        compiler_params=params(16),
        cost_estimate=pl.CostEstimate(flops=20_000_000_000, bytes_accessed=6_000_000, transcendentals=0),
        name="column",
    )(place, *column, first_rows)
    tiles = pl.pallas_call(
        pairs_kernel,
        out_shape=jax.ShapeDtypeStruct((8, CHUNK, HALF), jnp.int16),
        in_specs=[SMEM] + [VMEM] * 4,
        out_specs=VMEM,
        scratch_shapes=[pltpu.VMEM((CHIP, NOB * AUX), jnp.bfloat16)] + ids_scratch(2),
        compiler_params=params(16),
        name="pairs",
    )(place, dense, dense_rows(both), first_rows, swap(along))
    arrived = lax.all_to_all(tiles, ("x", "c"), 0, 0, tiled=True)
    wide = jax.ShapeDtypeStruct((WIDE, CHIP), jnp.int16)
    messages = pl.pallas_call(
        middle_kernel,
        out_shape=[wide] * 2,
        in_specs=[SMEM, VMEM],
        out_specs=[VMEM] * 2,
        compiler_params=params(24),
        name="middle",
    )(place, arrived)
    half = jax.ShapeDtypeStruct((HALF, CHIP), jnp.float32)
    keep, send = pl.pallas_call(
        join_kernel,
        out_shape=[half] * 2,
        in_specs=[SMEM, VMEM, VMEM],
        out_specs=[VMEM] * 2,
        compiler_params=params(16),
        name="join",
    )(place, *[lax.ppermute(a, AXES, far_round(r)) for r, a in enumerate(messages)])
    return pl.pallas_call(
        last_kernel,
        out_shape=half,
        in_specs=[VMEM] * 2,
        out_specs=VMEM,
        compiler_params=params(16),
        name="last",
    )(keep, swap(send))


def solution(mesh):
    fine = Mesh(mesh.devices.reshape(4, 4, 4, 4, 2), AXES)
    blk, grp = ("y", "zl", "c"), ("x", "zh")
    placed = (P(blk, grp, None, None), P(), P(blk, grp), P(blk, grp))
    return jax.shard_map(shards, mesh=fine, in_specs=placed, out_specs=P(blk, grp), check_vma=False)
```

```python
import jax
import jax.numpy as jnp
from jax import lax
from jax.experimental import pallas as pl
from jax.experimental.pallas import tpu as pltpu
from jax.sharding import Mesh, PartitionSpec as P

AXES = ("x", "zh", "y", "zl", "c")
NOB = 16
SLOTS = 6
BS = 64
AUX = 256
RB = 2
HALF = RB * BS
CHIP = 2 * HALF
BODY = RB * SLOTS * BS
PAY = BODY + 16
TILE = HALF + 16
LEVELS = 32000.0
CROSS = (3, 2, 0, 1)
VMEM = pl.BlockSpec(memory_space=pltpu.VMEM)
SMEM = pl.BlockSpec(memory_space=pltpu.SMEM)
ANY = pl.BlockSpec(memory_space=pl.ANY)


def params(mib):
    return pltpu.CompilerParams(vmem_limit_bytes=mib * 1024 * 1024)


def contract_kernel(raw_hbm, metric_hbm, sig_ref, live_ref, out_ref, raw_ref, metric_ref, sems):
    copies = [
        pltpu.make_async_copy(metric_hbm, metric_ref, sems.at[0]),
        pltpu.make_async_copy(raw_hbm, raw_ref, sems.at[1]),
    ]
    for copy in copies:
        copy.start()
    lane = lax.broadcasted_iota(jnp.int32, (16, AUX), 1)
    ids = jnp.zeros((16, AUX), jnp.int32)
    for m in range(RB):
        for s in range(SLOTS):
            ids = jnp.where(lane == m * SLOTS + s, sig_ref[m, s], ids)
    out_ref[BODY:, :] = ids.astype(jnp.float32).astype(jnp.bfloat16)
    for copy in copies:
        copy.wait()
    for m in range(RB):
        for s in range(SLOTS):
            block = m * SLOTS + s
            product = jnp.dot(
                raw_ref[m, s], metric_ref[...], preferred_element_type=jnp.float32
            )
            live = (s < live_ref[m]).astype(jnp.float32)
            out_ref[block * BS : (block + 1) * BS, :] = (product * live).astype(jnp.bfloat16)


def encode(values):
    top = jnp.max(jnp.abs(values), axis=0, keepdims=True)
    exponent = jnp.ceil(jnp.log2(jnp.maximum(top, 1e-30)) + 1e-3)
    coded = jnp.round(values * (LEVELS * jnp.exp2(-exponent)))
    return coded.astype(jnp.int32).astype(jnp.int16), exponent.astype(jnp.int32)


def decode(coded, exponents, row):
    scale = jnp.exp2(exponents[row : row + 1, :].astype(jnp.float32)) * (1.0 / LEVELS)
    return coded.astype(jnp.int32).astype(jnp.float32) * scale


def pick_rows(rows, width):
    at = lax.broadcasted_iota(jnp.int32, (16, width), 0)
    block = jnp.zeros((16, width), jnp.int32)
    for i, row in enumerate(rows):
        block = jnp.where(at == i, jnp.broadcast_to(row, (16, width)), block)
    return block


def load_ids(sources, ids_vmem, ids_smem, sem):
    for i, src in enumerate(sources):
        ids = src[BODY:PAY, 0:128].astype(jnp.float32).astype(jnp.int32)
        ids_vmem[i] = ids[0:8, :]
    return pltpu.make_async_copy(ids_vmem, ids_smem, sem)


def scatter(src, ids, row, target, first):
    for m in range(RB):
        for s in range(SLOTS):
            block = m * SLOTS + s
            orbital = ids[row, 0, block]
            lanes = pl.ds(pl.multiple_of(orbital * AUX, AUX), AUX)
            rows = pl.ds(pl.multiple_of(first + m * BS, BS), BS)
            target[rows, lanes] = src[block * BS : (block + 1) * BS, :]


NT = (((1,), (1,)), ((), ()))


TYPES = 3
CHUNK = TYPES * CHIP + 16
PART = 2 * CHIP + 16
WIDE = CHIP + 16


def column_kernel(place_ref, *refs):
    column, (out_ref, ids_vmem, ids, sem) = refs[:4], refs[5:]
    copy = load_ids(column, ids_vmem, ids, sem)
    copy.start()
    out_ref[...] = jnp.zeros_like(out_ref)
    copy.wait()
    for i, d in enumerate((0, 2, 1, 3)):
        scatter(column[i], ids, i, out_ref, lax.rem(place_ref[0] + d, 4) * HALF)


def rows_kernel(src, out_ref, ids_vmem, ids, sem):
    halves = [src.at[k] for k in range(2)]
    copy = load_ids(halves, ids_vmem, ids, sem)
    copy.start()
    out_ref[...] = jnp.zeros_like(out_ref)
    copy.wait()
    for k in range(2):
        scatter(halves[k], ids, k, out_ref, k * HALF)


def pairs_kernel(place_ref, cols, own_rows, first_rows, src, out_ref, rows, ids_vmem, ids, sem):
    core = place_ref[1]
    rows_kernel(src, rows, ids_vmem, ids, sem)
    exponents = {}
    places = (0, (2 - core) * CHIP, (1 + core) * CHIP)
    for t, block in enumerate((own_rows, first_rows, rows)):
        part = lax.dot_general(block[...], cols[...], NT, preferred_element_type=jnp.float32)
        for i in range(4):
            coded, exponents[t, i] = encode(part[:, i * HALF : (i + 1) * HALF])
            at = pl.ds(places[t] if t == 0 else pl.multiple_of(places[t], CHIP), CHIP)
            out_ref[i, at, :] = coded
    zero = core == 0
    for i in range(4):
        near = jnp.where(zero, exponents[2, i], exponents[1, i])
        across = jnp.where(zero, exponents[1, i], exponents[2, i])
        block = pick_rows([exponents[0, i], near, across], HALF)
        out_ref[i, TYPES * CHIP :, :] = block.astype(jnp.int16)


def sum_kernel(place_ref, in_ref, keep_ref, send_ref):
    totals = []
    for t in range(TYPES):
        total = None
        for x in range(4):
            exps = in_ref[x, TYPES * CHIP :, :].astype(jnp.int32)
            value = decode(in_ref[x, t * CHIP : (t + 1) * CHIP, :], exps, t)
            total = value if total is None else total + value
        totals.append(total)
    zero = place_ref[1] == 0
    keep_ref[:CHIP, :] = jnp.where(zero, totals[0], totals[2])
    keep_ref[CHIP:, :] = totals[1]
    exponents = []
    for u, total in enumerate((jnp.where(zero, totals[2], totals[0]), totals[1])):
        coded, exponent = encode(total)
        send_ref[u * CHIP : (u + 1) * CHIP, :] = coded
        exponents.append(exponent)
    send_ref[2 * CHIP :, :] = pick_rows(exponents, HALF).astype(jnp.int16)


def middle_kernel(place_ref, keep_ref, come_ref, first_ref, second_ref):
    tiles = []
    zero = place_ref[1] == 0
    exps = come_ref[2 * CHIP :, :].astype(jnp.int32)
    for u in range(2):
        rows = slice(u * CHIP, (u + 1) * CHIP)
        kept, come = keep_ref[rows, :], decode(come_ref[rows, :], exps, u)
        halves = [jnp.where(zero, kept, come), jnp.where(zero, come, kept)]
        tiles.append(jnp.concatenate(halves, axis=1))
    first = encode(tiles[0])
    second = encode(jnp.where(place_ref[1] == 0, tiles[1], tiles[0].T))

    def write(ref, pair):
        ref[:CHIP, :] = pair[0]
        ref[CHIP:, :] = jnp.broadcast_to(pair[1], (16, CHIP)).astype(jnp.int16)

    z = place_ref[3]
    to = jnp.where(place_ref[1] == 0, z, jnp.where(z < 2, 3 - z, z - 2))
    far = lax.rem(place_ref[2] + 4 - to, 4) >= 2
    straight = jnp.logical_xor(far, place_ref[1] == 1)

    @pl.when(straight)
    def _():
        write(first_ref, first)
        write(second_ref, second)

    @pl.when(jnp.logical_not(straight))
    def _():
        write(first_ref, second)
        write(second_ref, first)


def join_kernel(place_ref, a_ref, b_ref, keep_ref, send_ref):
    core = place_ref[1]
    for ref, half in ((keep_ref, core), (send_ref, 1 - core)):
        rows = pl.ds(pl.multiple_of(half * HALF, HALF), HALF)
        ref[...] = sum(
            decode(src[rows, :], src[CHIP:, :].astype(jnp.int32), 0) for src in (a_ref, b_ref)
        )


def last_kernel(keep_ref, come_ref, out_ref):
    out_ref[...] = 0.25 * (keep_ref[...] + come_ref[...])


def index_of(x, zh, y, zl, c):
    return (((x * 4 + zh) * 4 + y) * 4 + zl) * 2 + c


def far_round(r):
    pairs = []
    for x in range(4):
        for s in range(4):
            for y in range(4):
                for z in range(4):
                    kinds = (
                        ((x, z, y, z), (x, z, y, z ^ 1)),
                        ((x, z, y, CROSS[z]), (y, CROSS[z], x, z)),
                    )
                    for c in range(2):
                        away = (s - (CROSS[z] if c else z)) % 4
                        straight = (away >= 2) != (c == 1)
                        dest = kinds[c][r if straight else 1 - r]
                        pairs.append((index_of(x, s, y, z, c), index_of(*dest, away % 2)))
    return pairs


def shards(raw_blocks, metric_factor, sig_list, live_count):
    place = jnp.stack([lax.axis_index("y"), lax.axis_index("c"), lax.axis_index("zh"), lax.axis_index("zl")])
    place = place.astype(jnp.int32)
    own = pl.pallas_call(
        contract_kernel,
        out_shape=jax.ShapeDtypeStruct((PAY, AUX), jnp.bfloat16),
        in_specs=[ANY, ANY, SMEM, SMEM],
        out_specs=VMEM,
        scratch_shapes=[
            pltpu.VMEM(raw_blocks.shape, jnp.bfloat16),
            pltpu.VMEM((AUX, AUX), jnp.bfloat16),
            pltpu.SemaphoreType.DMA((2,)),
        ],
        compiler_params=params(56),
        name="contract",
    )(raw_blocks, metric_factor, sig_list, live_count.reshape(RB))

    def swap(a):
        return lax.ppermute(a, "c", [(0, 1), (1, 0)])

    both = lax.all_gather(own, "c")
    along = lax.ppermute(
        both,
        ("zl", "c"),
        [(CROSS[i] * 2, i * 2) for i in range(4)] + [((i ^ 1) * 2 + 1, i * 2 + 1) for i in range(4)],
    )
    column = [own] + [lax.ppermute(own, "y", [((i + d) % 4, i) for i in range(4)]) for d in (2, 1, 3)]
    def ids_scratch(count):
        return [
            pltpu.VMEM((count, 8, 128), jnp.int32),
            pltpu.SMEM((count, 8, 128), jnp.int32),
            pltpu.SemaphoreType.DMA,
        ]

    def dense_rows(block):
        return pl.pallas_call(
            rows_kernel,
            out_shape=jax.ShapeDtypeStruct((CHIP, NOB * AUX), jnp.bfloat16),
            in_specs=[VMEM],
            out_specs=VMEM,
            scratch_shapes=ids_scratch(2),
            compiler_params=params(16),
            cost_estimate=pl.CostEstimate(flops=1_000_000_000, bytes_accessed=3_000_000, transcendentals=0),
            name="rows",
        )(block)

    first_rows = dense_rows(along)
    dense = pl.pallas_call(
        column_kernel,
        out_shape=jax.ShapeDtypeStruct((4 * HALF, NOB * AUX), jnp.bfloat16),
        in_specs=[SMEM] + [VMEM] * 4 + [ANY],
        out_specs=VMEM,
        scratch_shapes=ids_scratch(4),
        compiler_params=params(16),
        cost_estimate=pl.CostEstimate(flops=20_000_000_000, bytes_accessed=6_000_000, transcendentals=0),
        name="column",
    )(place, *column, first_rows)
    tiles = pl.pallas_call(
        pairs_kernel,
        out_shape=jax.ShapeDtypeStruct((4, CHUNK, HALF), jnp.int16),
        in_specs=[SMEM] + [VMEM] * 4,
        out_specs=VMEM,
        scratch_shapes=[pltpu.VMEM((CHIP, NOB * AUX), jnp.bfloat16)] + ids_scratch(2),
        compiler_params=params(16),
        name="pairs",
    )(place, dense, dense_rows(both), first_rows, swap(along))
    arrived = lax.all_to_all(tiles, "x", 0, 0, tiled=True)
    kept, part = pl.pallas_call(
        sum_kernel,
        out_shape=[
            jax.ShapeDtypeStruct((2 * CHIP, HALF), jnp.float32),
            jax.ShapeDtypeStruct((PART, HALF), jnp.int16),
        ],
        in_specs=[SMEM, VMEM],
        out_specs=[VMEM] * 2,
        compiler_params=params(24),
        name="sum",
    )(place, arrived)
    wide = jax.ShapeDtypeStruct((WIDE, CHIP), jnp.int16)
    messages = pl.pallas_call(
        middle_kernel,
        out_shape=[wide] * 2,
        in_specs=[SMEM, VMEM, VMEM],
        out_specs=[VMEM] * 2,
        compiler_params=params(24),
        name="middle",
    )(place, kept, swap(part))
    half = jax.ShapeDtypeStruct((HALF, CHIP), jnp.float32)
    keep, send = pl.pallas_call(
        join_kernel,
        out_shape=[half] * 2,
        in_specs=[SMEM, VMEM, VMEM],
        out_specs=[VMEM] * 2,
        compiler_params=params(16),
        name="join",
    )(place, *[lax.ppermute(a, AXES, far_round(r)) for r, a in enumerate(messages)])
    return pl.pallas_call(
        last_kernel,
        out_shape=half,
        in_specs=[VMEM] * 2,
        out_specs=VMEM,
        compiler_params=params(16),
        name="last",
    )(keep, swap(send))


def solution(mesh):
    fine = Mesh(mesh.devices.reshape(4, 4, 4, 4, 2), AXES)
    blk, grp = ("y", "zl", "c"), ("x", "zh")
    placed = (P(blk, grp, None, None), P(), P(blk, grp), P(blk, grp))
    return jax.shard_map(shards, mesh=fine, in_specs=placed, out_specs=P(blk, grp), check_vma=False)
```

```python
import jax
import jax.numpy as jnp
from jax import lax
from jax.experimental import pallas as pl
from jax.experimental.pallas import tpu as pltpu
from jax.sharding import Mesh, PartitionSpec as P

AXES = ("x", "zh", "y", "zl", "c")
NOB = 16
SLOTS = 6
BS = 64
AUX = 256
RB = 2
HALF = RB * BS
CHIP = 2 * HALF
BODY = RB * SLOTS * BS
PAY = BODY + 16
TILE = HALF + 16
LEVELS = 32000.0
CROSS = (3, 2, 0, 1)
VMEM = pl.BlockSpec(memory_space=pltpu.VMEM)
SMEM = pl.BlockSpec(memory_space=pltpu.SMEM)
ANY = pl.BlockSpec(memory_space=pl.ANY)


def params(mib):
    return pltpu.CompilerParams(vmem_limit_bytes=mib * 1024 * 1024)


def contract_kernel(raw_hbm, metric_hbm, sig_ref, live_ref, out_ref, raw_ref, metric_ref, sems):
    copies = [
        pltpu.make_async_copy(metric_hbm, metric_ref, sems.at[0]),
        pltpu.make_async_copy(raw_hbm, raw_ref, sems.at[1]),
    ]
    for copy in copies:
        copy.start()
    lane = lax.broadcasted_iota(jnp.int32, (16, AUX), 1)
    ids = jnp.zeros((16, AUX), jnp.int32)
    for m in range(RB):
        for s in range(SLOTS):
            ids = jnp.where(lane == m * SLOTS + s, sig_ref[m, s], ids)
    out_ref[BODY:, :] = ids.astype(jnp.float32).astype(jnp.bfloat16)
    for copy in copies:
        copy.wait()
    for m in range(RB):
        for s in range(SLOTS):
            block = m * SLOTS + s
            product = jnp.dot(
                raw_ref[m, s], metric_ref[...], preferred_element_type=jnp.float32
            )
            live = (s < live_ref[m]).astype(jnp.float32)
            out_ref[block * BS : (block + 1) * BS, :] = (product * live).astype(jnp.bfloat16)


def encode(values):
    top = jnp.max(jnp.abs(values), axis=0, keepdims=True)
    exponent = jnp.ceil(jnp.log2(jnp.maximum(top, 1e-30)) + 1e-3)
    coded = jnp.round(values * (LEVELS * jnp.exp2(-exponent)))
    return coded.astype(jnp.int32).astype(jnp.int16), exponent.astype(jnp.int32)


def decode(coded, exponents, row):
    scale = jnp.exp2(exponents[row : row + 1, :].astype(jnp.float32)) * (1.0 / LEVELS)
    return coded.astype(jnp.int32).astype(jnp.float32) * scale


def pick_rows(rows, width):
    at = lax.broadcasted_iota(jnp.int32, (16, width), 0)
    block = jnp.zeros((16, width), jnp.int32)
    for i, row in enumerate(rows):
        block = jnp.where(at == i, jnp.broadcast_to(row, (16, width)), block)
    return block


def load_ids(sources, ids_vmem, ids_smem, sem):
    for i, src in enumerate(sources):
        ids = src[BODY:PAY, 0:128].astype(jnp.float32).astype(jnp.int32)
        ids_vmem[i] = ids[0:8, :]
    return pltpu.make_async_copy(ids_vmem, ids_smem, sem)


def scatter(src, ids, row, target, first):
    for m in range(RB):
        for s in range(SLOTS):
            block = m * SLOTS + s
            orbital = ids[row, 0, block]
            lanes = pl.ds(pl.multiple_of(orbital * AUX, AUX), AUX)
            rows = pl.ds(pl.multiple_of(first + m * BS, BS), BS)
            target[rows, lanes] = src[block * BS : (block + 1) * BS, :]


NT = (((1,), (1,)), ((), ()))


TYPES = 3
CHUNK = 2 * CHIP + 16
WIDE = CHIP + 16


def column_kernel(place_ref, *refs):
    column, (out_ref, ids_vmem, ids, sem) = refs[:4], refs[5:]
    copy = load_ids(column, ids_vmem, ids, sem)
    copy.start()
    out_ref[...] = jnp.zeros_like(out_ref)
    copy.wait()
    for i, d in enumerate((0, 1, 3, 2)):
        scatter(column[i], ids, i, out_ref, lax.rem(place_ref[0] + d, 4) * HALF)


def rows_kernel(src, out_ref, ids_vmem, ids, sem):
    halves = [src.at[k] for k in range(2)]
    copy = load_ids(halves, ids_vmem, ids, sem)
    copy.start()
    out_ref[...] = jnp.zeros_like(out_ref)
    copy.wait()
    for k in range(2):
        scatter(halves[k], ids, k, out_ref, k * HALF)


def pairs_kernel(place_ref, cols, own_rows, first_rows, src, out_ref, rows, ids_vmem, ids, sem):
    core = place_ref[1]
    rows_kernel(src, rows, ids_vmem, ids, sem)
    exponents = {}
    places = ((0, 0), (1 - core, core * CHIP), (core, (1 - core) * CHIP))
    for t, block in enumerate((own_rows, first_rows, rows)):
        part = lax.dot_general(block[...], cols[...], NT, preferred_element_type=jnp.float32)
        chunk, first = places[t]
        for i in range(4):
            coded, exponents[t, i] = encode(part[:, i * HALF : (i + 1) * HALF])
            at = pl.ds(first if t == 0 else pl.multiple_of(first, CHIP), CHIP)
            out_ref[i * 2 + chunk, at, :] = coded
    zero = core == 0
    for i in range(4):
        out_ref[i * 2 + 1, CHIP : 2 * CHIP, :] = jnp.zeros((CHIP, HALF), jnp.int16)
        near = jnp.where(zero, exponents[2, i], exponents[1, i])
        across = jnp.where(zero, exponents[1, i], exponents[2, i])
        out_ref[i * 2, 2 * CHIP :, :] = pick_rows([exponents[0, i], near], HALF).astype(jnp.int16)
        out_ref[i * 2 + 1, 2 * CHIP :, :] = pick_rows([across], HALF).astype(jnp.int16)


def middle_kernel(place_ref, in_ref, first_ref, second_ref):
    tiles = []
    for u in range(2):
        halves = []
        for k in range(2):
            total = None
            for x in range(4):
                exps = in_ref[x * 2 + k, 2 * CHIP :, :].astype(jnp.int32)
                value = decode(in_ref[x * 2 + k, u * CHIP : (u + 1) * CHIP, :], exps, u)
                total = value if total is None else total + value
            halves.append(total)
        tiles.append(jnp.concatenate(halves, axis=1))
    first = encode(tiles[0])
    second = encode(jnp.where(place_ref[1] == 0, tiles[1], tiles[0].T))

    def write(ref, pair):
        ref[:CHIP, :] = pair[0]
        ref[CHIP:, :] = jnp.broadcast_to(pair[1], (16, CHIP)).astype(jnp.int16)

    z = place_ref[3]
    to = jnp.where(place_ref[1] == 0, z, jnp.where(z < 2, 3 - z, z - 2))
    far = lax.rem(place_ref[2] + 4 - to, 4) >= 2
    straight = jnp.logical_xor(far, place_ref[1] == 1)

    @pl.when(straight)
    def _():
        write(first_ref, first)
        write(second_ref, second)

    @pl.when(jnp.logical_not(straight))
    def _():
        write(first_ref, second)
        write(second_ref, first)


def join_kernel(place_ref, a_ref, b_ref, keep_ref, send_ref):
    core = place_ref[1]
    for ref, half in ((keep_ref, core), (send_ref, 1 - core)):
        rows = pl.ds(pl.multiple_of(half * HALF, HALF), HALF)
        ref[...] = sum(
            decode(src[rows, :], src[CHIP:, :].astype(jnp.int32), 0) for src in (a_ref, b_ref)
        )


def last_kernel(keep_ref, come_ref, out_ref):
    out_ref[...] = 0.25 * (keep_ref[...] + come_ref[...])


def index_of(x, zh, y, zl, c):
    return (((x * 4 + zh) * 4 + y) * 4 + zl) * 2 + c


def far_round(r):
    pairs = []
    for x in range(4):
        for s in range(4):
            for y in range(4):
                for z in range(4):
                    kinds = (
                        ((x, z, y, z), (x, z, y, z ^ 1)),
                        ((x, z, y, CROSS[z]), (y, CROSS[z], x, z)),
                    )
                    for c in range(2):
                        away = (s - (CROSS[z] if c else z)) % 4
                        straight = (away >= 2) != (c == 1)
                        dest = kinds[c][r if straight else 1 - r]
                        pairs.append((index_of(x, s, y, z, c), index_of(*dest, away % 2)))
    return pairs


def shards(raw_blocks, metric_factor, sig_list, live_count):
    place = jnp.stack([lax.axis_index("y"), lax.axis_index("c"), lax.axis_index("zh"), lax.axis_index("zl")])
    place = place.astype(jnp.int32)
    own = pl.pallas_call(
        contract_kernel,
        out_shape=jax.ShapeDtypeStruct((PAY, AUX), jnp.bfloat16),
        in_specs=[ANY, ANY, SMEM, SMEM],
        out_specs=VMEM,
        scratch_shapes=[
            pltpu.VMEM(raw_blocks.shape, jnp.bfloat16),
            pltpu.VMEM((AUX, AUX), jnp.bfloat16),
            pltpu.SemaphoreType.DMA((2,)),
        ],
        compiler_params=params(56),
        name="contract",
    )(raw_blocks, metric_factor, sig_list, live_count.reshape(RB))

    def swap(a):
        return lax.ppermute(a, "c", [(0, 1), (1, 0)])

    both = lax.all_gather(own, "c")
    along = lax.ppermute(
        both,
        ("zl", "c"),
        [(CROSS[i] * 2, i * 2) for i in range(4)] + [((i ^ 1) * 2 + 1, i * 2 + 1) for i in range(4)],
    )
    column = [own] + [lax.ppermute(own, "y", [((i + d) % 4, i) for i in range(4)]) for d in (1, 3, 2)]
    def ids_scratch(count):
        return [
            pltpu.VMEM((count, 8, 128), jnp.int32),
            pltpu.SMEM((count, 8, 128), jnp.int32),
            pltpu.SemaphoreType.DMA,
        ]

    def dense_rows(block):
        return pl.pallas_call(
            rows_kernel,
            out_shape=jax.ShapeDtypeStruct((CHIP, NOB * AUX), jnp.bfloat16),
            in_specs=[VMEM],
            out_specs=VMEM,
            scratch_shapes=ids_scratch(2),
            compiler_params=params(16),
            cost_estimate=pl.CostEstimate(flops=1_000_000_000, bytes_accessed=3_000_000, transcendentals=0),
            name="rows",
        )(block)

    first_rows = dense_rows(along)
    dense = pl.pallas_call(
        column_kernel,
        out_shape=jax.ShapeDtypeStruct((4 * HALF, NOB * AUX), jnp.bfloat16),
        in_specs=[SMEM] + [VMEM] * 4 + [ANY],
        out_specs=VMEM,
        scratch_shapes=ids_scratch(4),
        compiler_params=params(16),
        cost_estimate=pl.CostEstimate(flops=20_000_000_000, bytes_accessed=6_000_000, transcendentals=0),
        name="column",
    )(place, *column, first_rows)
    tiles = pl.pallas_call(
        pairs_kernel,
        out_shape=jax.ShapeDtypeStruct((8, CHUNK, HALF), jnp.int16),
        in_specs=[SMEM] + [VMEM] * 4,
        out_specs=VMEM,
        scratch_shapes=[pltpu.VMEM((CHIP, NOB * AUX), jnp.bfloat16)] + ids_scratch(2),
        compiler_params=params(16),
        name="pairs",
    )(place, dense, dense_rows(both), first_rows, swap(along))
    arrived = lax.all_to_all(tiles, ("x", "c"), 0, 0, tiled=True)
    wide = jax.ShapeDtypeStruct((WIDE, CHIP), jnp.int16)
    messages = pl.pallas_call(
        middle_kernel,
        out_shape=[wide] * 2,
        in_specs=[SMEM, VMEM],
        out_specs=[VMEM] * 2,
        compiler_params=params(24),
        name="middle",
    )(place, arrived)
    half = jax.ShapeDtypeStruct((HALF, CHIP), jnp.float32)
    keep, send = pl.pallas_call(
        join_kernel,
        out_shape=[half] * 2,
        in_specs=[SMEM, VMEM, VMEM],
        out_specs=[VMEM] * 2,
        compiler_params=params(16),
        name="join",
    )(place, *[lax.ppermute(a, AXES, far_round(r)) for r, a in enumerate(messages)])
    return pl.pallas_call(
        last_kernel,
        out_shape=half,
        in_specs=[VMEM] * 2,
        out_specs=VMEM,
        compiler_params=params(16),
        name="last",
    )(keep, swap(send))


def solution(mesh):
    fine = Mesh(mesh.devices.reshape(4, 4, 4, 4, 2), AXES)
    blk, grp = ("y", "zl", "c"), ("x", "zh")
    placed = (P(blk, grp, None, None), P(), P(blk, grp), P(blk, grp))
    return jax.shard_map(shards, mesh=fine, in_specs=placed, out_specs=P(blk, grp), check_vma=False)
```
